32 devices in a mesh: groups: 2 (over y), gx: 4 (over z), gy: 2 (over x), lev: 2 (over core).
Axes of the slice: x: 2, y: 2, z: 4, core: 2. Of those that a mesh axis runs over, the one named last changes fastest.
Arguments:
- anomaly_codes: bfloat16 [40, 4, 128, 256], P(None, 'lev', ('groups', 'gx'), 'gy'), parts along dimension 2, may hold values from -127 to 127
- block_scales: float32 [40, 4, 128, 2], P(None, 'lev', ('groups', 'gx'), 'gy'), parts along dimension 2, may hold values from 0.004 to 0.04
- background: float32 [4, 128, 256], P('lev', ('groups', 'gx'), 'gy'), parts along dimension 1, may hold values from -6 to 6
- obs_values: float32 [8, 2, 128], P(('groups', 'gx'), 'gy'), parts along dimension 0, may hold values from -12 to 12
- obs_error: float32 [8, 2, 128], P(('groups', 'gx'), 'gy'), parts along dimension 0, may hold values from 0.2 to 2
- obs_cell: int32 [8, 2, 128], P(('groups', 'gx'), 'gy'), parts along dimension 0, may hold values from 0 to 2047
- obs_level: int32 [8, 2, 128], P(('groups', 'gx'), 'gy'), parts along dimension 0, may hold values from 0 to 3
- obs_count: int32 [8, 2], P(('groups', 'gx'), 'gy'), parts along dimension 0, may hold values from 64 to 128, as said below
- conv1_weight: float32 [3, 3, 8, 32], replicated, may hold values from -0.75 to 0.75
- conv1_bias: float32 [32], replicated, may hold values from -3 to 3
- conv2_weight: float32 [3, 3, 32, 32], replicated, may hold values from -0.375 to 0.375
- conv2_bias: float32 [32], replicated, may hold values from -3 to 3
- head_weight: float32 [32], replicated, may hold values from -1 to 1
- head_bias: float32 [1], replicated, may hold values from -3 to 3
Outputs:
- increment: float32 [4, 128, 256], P('lev', ('groups', 'gx'), 'gy'), parts along dimension 1
- taper_field: float32 [128, 256], P(('groups', 'gx'), 'gy'), parts along dimension 0
The draws below stay inside these ranges and needn't reach their ends.
There are 2 independent parts, one for each index of `groups`. The reference program is written for one: setup_inputs(seed, part) draws one part's arguments, and reference() takes and returns one part's arrays. A program takes and returns all parts, laid end to end along the dimension named above; an argument that names none is the same for every part. Nothing has to cross between parts.
Inputs may be any that keep to these rules, and one draw needn't show every extreme that they name: `obs_count`: in every draw at least one tile uses all 128 slots.
All inputs are finite; a program needn't handle non-finite values.
Results may differ from the reference program's by a relative error of at most 0.0003.
The reference program's roundings to bfloat16 on the way (of `coefficients` and `localization`) count: a program that leaves them out, or rounds other values in their place, can miss the bound.
Values may be sent and summed in bfloat16 or wider, within the bound.
A program may use at most 64 MiB of HBM per device.

```python
import math
import jax
import jax.numpy as jnp
from jax import lax

MEMBERS = 40
TX = 16
TY = 128
OBS_TILE = 128
FEAT = 8
CH = 32
STEP = 2
VCUT = 6
CUT = 6
LEVELS = 4
NX = 64
NY = 256
TILES_X = 4
TILES_Y = 2


def draw_obs_values(key, part):
    key = jax.random.fold_in(key, 11)
    draw_shape = (TILES_X, TILES_Y, OBS_TILE)
    rise_rows = 1.0 + 2.0 * jnp.arange(TILES_X, dtype=jnp.float32) / max(TILES_X - 1, 1)
    values_base = jnp.clip(jax.random.normal(key, draw_shape, jnp.float32), -4.0, 4.0)
    return values_base * rise_rows[:, None, None]


def draw_obs_count(key, part):
    key = jax.random.fold_in(key, 23)
    first_key, second_key = jax.random.split(key)
    counts = jax.random.randint(first_key, (TILES_X, TILES_Y), OBS_TILE // 2, OBS_TILE + 1)
    full_tile = jax.random.randint(second_key, (), 0, TILES_X * TILES_Y)
    positions = jnp.arange(TILES_X * TILES_Y, dtype=jnp.int32).reshape(TILES_X, TILES_Y)
    return jnp.where(positions == full_tile, OBS_TILE, counts).astype(jnp.int32)


def plant(drawn, stream_key, least, high):
    longest = drawn.shape.index(max(drawn.shape))
    spots = []
    for shift in (0, 1):
        where = [jax.random.randint(jax.random.fold_in(stream_key, axis), (), 0, length) for axis, length in enumerate(drawn.shape)]
        where[longest] = (where[longest] + shift) % drawn.shape[longest]
        spots.append(tuple(where))
    return drawn.at[spots[0]].set(least).at[spots[1]].set(high)


def steps_of(rng, shape, cuts, smallest, top_value):
    def one(axis_at, shards_of):
        draws = jax.random.uniform(jax.random.fold_in(jax.random.fold_in(rng, 6), axis_at), (shards_of,), jnp.float32, smallest / len(cuts), top_value / len(cuts))
        return jnp.repeat(jnp.exp(draws), shape[axis_at] // shards_of).reshape((-1,) + (1,) * (len(shape) - axis_at - 1))

    factor_of = one(*cuts[0])
    for cut in cuts[1:]:
        factor_of = factor_of * one(*cut)
    return factor_of


def gaussian(stream_key, shape, scale, limit, shards=(), kind=jnp.bfloat16):
    result = jax.random.normal(stream_key, shape, jnp.float32) * scale
    if len(shards) > 0:
        result = steps_of(stream_key, shape, shards, -0.22, 0.18) * result
    return jnp.clip(result, min=-limit, max=limit).astype(kind)


def setup_inputs(seed: int = 0, part: int = 0) -> dict:
    splits = jax.random.split(jax.random.key(seed), 15)
    part_splits = jax.random.split(jax.random.fold_in(splits[14], part), 15)
    anomaly_codes = jnp.clip(jax.random.uniform(part_splits[0], (MEMBERS, LEVELS, NX, NY), jnp.float32, -127.0, 127.0) * steps_of(part_splits[0], (MEMBERS, LEVELS, NX, NY), ((1, 2), (2, 4), (3, 2)), -0.4, 0.0), -127.0, 127.0).astype(jnp.bfloat16)
    block_scales = jnp.clip(jnp.exp(math.log(0.04) - 2.30258502 * jax.random.uniform(part_splits[1], (MEMBERS, LEVELS, NX, NY // 128), jnp.float32) ** steps_of(part_splits[1], (MEMBERS, LEVELS, NX, NY // 128), ((1, 2), (2, 4), (3, 2)), -0.2, 0.2)), 0.004, 0.04)
    background = gaussian(part_splits[2], (LEVELS, NX, NY), 1.0, 6.0, ((0, 2), (1, 4), (2, 2)), jnp.float32)
    obs_values = draw_obs_values(jax.random.fold_in(jax.random.fold_in(splits[14], part), 71), part)
    obs_error = jnp.clip(jnp.exp(math.log(2.0) - 2.3025851 * jax.random.uniform(part_splits[4], (TILES_X, TILES_Y, OBS_TILE), jnp.float32) ** steps_of(part_splits[4], (TILES_X, TILES_Y, OBS_TILE), ((0, 4), (1, 2)), -0.2, 0.2)), 0.2, 2.0)
    obs_cell = plant(jax.random.randint(part_splits[5], (TILES_X, TILES_Y, OBS_TILE), 0, TX * TY), jax.random.fold_in(part_splits[5], 1), 0, (TX * TY) - 1).astype(jnp.int32)
    obs_level = plant(jax.random.randint(part_splits[6], (TILES_X, TILES_Y, OBS_TILE), 0, LEVELS), jax.random.fold_in(part_splits[6], 1), 0, LEVELS - 1).astype(jnp.int32)
    obs_count = draw_obs_count(jax.random.fold_in(jax.random.fold_in(splits[14], part), 71), part)
    conv1_weight = gaussian(splits[8], (3, 3, FEAT, CH), (9 * FEAT) ** -0.5, 0.75, (), jnp.float32)
    conv1_bias = gaussian(splits[9], (CH,), 0.5, 3.0, (), jnp.float32)
    conv2_weight = gaussian(splits[10], (3, 3, CH, CH), (9 * CH) ** -0.5, 0.375, (), jnp.float32)
    conv2_bias = gaussian(splits[11], (CH,), 0.5, 3.0, (), jnp.float32)
    head_weight = gaussian(splits[12], (CH,), CH ** -0.5, 1.0, (), jnp.float32)
    head_bias = gaussian(splits[13], (1,), 1.0, 3.0, (), jnp.float32)
    return dict(anomaly_codes=anomaly_codes, block_scales=block_scales, background=background, obs_values=obs_values, obs_error=obs_error, obs_cell=obs_cell, obs_level=obs_level, obs_count=obs_count, conv1_weight=conv1_weight, conv1_bias=conv1_bias, conv2_weight=conv2_weight, conv2_bias=conv2_bias, head_weight=head_weight, head_bias=head_bias)


unit_moves = ((-1, -1), (-1, 0), (-1, 1), (0, -1), (0, 1), (1, -1), (1, 0), (1, 1))
epsilon = 1e-06
highest = lax.Precision.HIGHEST

def same_conv(inputs, kernel):
    return lax.conv_general_dilated(inputs[None], kernel, (1, 1), 'SAME', dimension_numbers=('NCHW', 'HWIO', 'NCHW'), precision=highest)[0]

def vertical_taper(level_one, level_two):
    ratio = (level_one - level_two) / VCUT
    return jnp.square(jnp.maximum(0.0, 1.0 - ratio * ratio))

def reference(anomaly_codes, block_scales, background, obs_values, obs_error, obs_cell, obs_level, obs_count, conv1_weight, conv1_bias, conv2_weight, conv2_bias, head_weight, head_bias):
    weight_total = float(MEMBERS * LEVELS)

    def member_terms(running, member_index):
        squares, products = running
        member = anomaly_codes[member_index].astype(jnp.float32) * jnp.repeat(block_scales[member_index], 128, axis=2)
        padded = jnp.pad(member, ((0, 0), (STEP, STEP), (STEP, STEP)))
        squares = squares + lax.optimization_barrier(jnp.sum(padded * padded, axis=0)) / weight_total
        shifted_terms = []
        for offset in unit_moves:
            row_from = STEP + offset[0] * STEP
            col_from = STEP + offset[1] * STEP
            shifted = padded[:, row_from:row_from + NX, col_from:col_from + NY]
            shifted_terms.append(lax.optimization_barrier(jnp.sum(member * shifted, axis=0)) / weight_total)
        return ((squares, products + jnp.stack(shifted_terms)), None)
    start_state = (jnp.zeros((NX + 2 * STEP, NY + 2 * STEP), jnp.float32), jnp.zeros((FEAT, NX, NY), jnp.float32))
    (squares, products), unused = lax.scan(member_terms, start_state, jnp.arange(MEMBERS, dtype=jnp.int32))
    centre = squares[STEP:STEP + NX, STEP:STEP + NY]
    channels = []
    for position, offset in enumerate(unit_moves):
        row_from = STEP + offset[0] * STEP
        col_from = STEP + offset[1] * STEP
        shifted = squares[row_from:row_from + NX, col_from:col_from + NY]
        channels.append(products[position] / jnp.sqrt((centre + epsilon) * (shifted + epsilon)))
    features = jnp.stack(channels)
    hidden = jax.nn.relu(same_conv(features, conv1_weight) + conv1_bias[:, None, None])
    hidden = jax.nn.relu(same_conv(hidden, conv2_weight) + conv2_bias[:, None, None])
    taper_field = jax.nn.sigmoid(jnp.einsum('cxy,c->xy', hidden, head_weight, precision=highest) + head_bias[0])
    tile_rows = jnp.arange(TILES_X, dtype=jnp.int32)[:, None, None]
    tile_cols = jnp.arange(TILES_Y, dtype=jnp.int32)[None, :, None]
    local_rows = obs_cell // TY
    local_cols = obs_cell % TY
    grid_rows = tile_rows * TX + local_rows
    grid_cols = tile_cols * TY + local_cols
    obs_anom = anomaly_codes[:, obs_level, grid_rows, grid_cols].astype(jnp.float32) * block_scales[:, obs_level, grid_rows, grid_cols // 128]
    obs_mean = background[obs_level, grid_rows, grid_cols]
    usable = jnp.arange(OBS_TILE, dtype=jnp.int32)[None, None, :] < obs_count[:, :, None]
    misfit = obs_values - obs_mean
    spread = lax.optimization_barrier(jnp.sum(obs_anom * obs_anom, axis=0)) / (MEMBERS - 1)
    misfit_total = jnp.sum(jnp.where(usable, misfit * misfit, 0.0))
    spread_total = jnp.sum(jnp.where(usable, spread, 0.0))
    error_total = jnp.sum(jnp.where(usable, obs_error, 0.0))
    inflation = misfit_total / (spread_total + error_total)
    obs_gain = jnp.where(usable, misfit / (inflation * spread + obs_error), 0.0)
    obs_weight = taper_field[grid_rows, grid_cols] * obs_gain / (MEMBERS - 1)
    level_values = jnp.arange(LEVELS, dtype=jnp.int32).astype(jnp.float32)[:, None, None, None]
    vertical = vertical_taper(level_values, obs_level.astype(jnp.float32)[None])
    coefficients = ((vertical * obs_weight[None])[:, None] * obs_anom[None]).astype(jnp.bfloat16)
    coeff_padded = jnp.pad(coefficients, ((0, 0), (0, 0), (1, 1), (1, 1), (0, 0)))
    rows_padded = jnp.pad(local_rows, ((1, 1), (1, 1), (0, 0)))
    cols_padded = jnp.pad(local_cols, ((1, 1), (1, 1), (0, 0)))
    cell_rows = jnp.arange(TX * TY, dtype=jnp.int32) // TY
    cell_cols = jnp.arange(TX * TY, dtype=jnp.int32) % TY
    shift_three = jnp.arange(3, dtype=jnp.int32) - 1

    def tile_update(tile_index):
        row_tile = tile_index // TILES_Y
        col_tile = tile_index % TILES_Y
        zero_index = jnp.zeros((), jnp.int32)
        block = lax.dynamic_slice(coeff_padded, (zero_index, zero_index, row_tile, col_tile, zero_index), (LEVELS, MEMBERS, 3, 3, OBS_TILE))
        coeff_matrix = block.reshape(LEVELS * MEMBERS, 9 * OBS_TILE).T
        near_rows = lax.dynamic_slice(rows_padded, (row_tile, col_tile, zero_index), (3, 3, OBS_TILE)) + shift_three[:, None, None] * TX
        near_cols = lax.dynamic_slice(cols_padded, (row_tile, col_tile, zero_index), (3, 3, OBS_TILE)) + shift_three[None, :, None] * TY
        row_gap = (cell_rows[:, None] - near_rows.reshape(-1)[None, :]).astype(jnp.float32)
        col_gap = (cell_cols[:, None] - near_cols.reshape(-1)[None, :]).astype(jnp.float32)
        distance = row_gap * row_gap + col_gap * col_gap
        localization = jnp.square(jnp.maximum(0.0, 1.0 - distance / (CUT * CUT))).astype(jnp.bfloat16)
        weights = jnp.dot(localization, coeff_matrix, preferred_element_type=jnp.float32).reshape(TX * TY, LEVELS, MEMBERS)
        code_tile = lax.dynamic_slice(anomaly_codes, (zero_index, zero_index, row_tile * TX, col_tile * TY), (MEMBERS, LEVELS, TX, TY))
        scale_tile = lax.dynamic_slice(block_scales, (zero_index, zero_index, row_tile * TX, col_tile * (TY // 128)), (MEMBERS, LEVELS, TX, TY // 128))
        tile_anom = (code_tile.astype(jnp.float32) * jnp.repeat(scale_tile, 128, axis=3)).reshape(MEMBERS, LEVELS, TX * TY)
        combined = jnp.einsum('mlc,clm->lc', tile_anom, weights, precision=highest)
        taper_tile = lax.dynamic_slice(taper_field, (row_tile * TX, col_tile * TY), (TX, TY)).reshape(TX * TY)
        return (inflation * taper_tile * combined).reshape(LEVELS, TX, TY)
    pieces = lax.map(tile_update, jnp.arange(TILES_X * TILES_Y, dtype=jnp.int32))
    increment = pieces.reshape(TILES_X, TILES_Y, LEVELS, TX, TY).transpose(2, 0, 3, 1, 4).reshape(LEVELS, NX, NY)
    return (increment, taper_field)
```

```python
import functools

import jax
import jax.numpy as jnp
from jax import lax
from jax.experimental import pallas as pl
from jax.experimental.pallas import tpu as pltpu
from jax.sharding import PartitionSpec as P

STEP = 2
VCUT = 6
CUT = 6
RIM = 4
EPS = 1e-06
MOVES = ((-1, -1), (-1, 0), (-1, 1), (0, -1), (0, 1), (1, -1), (1, 0), (1, 1))
MESH = pl.DeviceIdType.MESH
F32 = jnp.float32
BF16 = jnp.bfloat16


def split_two(x):
    high = x.astype(BF16)
    return high, (x - high.astype(F32)).astype(BF16)


def split_three(x):
    high = x.astype(BF16)
    rest = x - high.astype(F32)
    middle = rest.astype(BF16)
    return high, middle, (rest - middle.astype(F32)).astype(BF16)


def dot(a, b, ca=1, cb=0):
    return lax.dot_general(a, b, (((ca,), (cb,)), ((), ())), preferred_element_type=F32)


def kernel(
    gxn,
    gyn,
    members,
    a_in,
    back_ref,
    obs_ref,
    wts_ref,
    inc_ref,
    taper_ref,
    main,
    ext,
    ecol,
    erecv,
    opart,
    opeer,
    opack,
    orecv,
    sums,
    speer,
    wown,
    wrecv,
    stat,
    srecv,
    feat,
    hid,
    near,
    coef,
    halo_send,
    halo_recv,
    obs_send,
    obs_recv,
    wt_send,
    wt_recv,
    st_send,
    st_recv,
    lev_send,
    lev_recv,
):
    rows, both, cols = a_in.shape
    total_levels = 2 * 2
    g = lax.axis_index("groups")
    gx = lax.axis_index("gx")
    gy = lax.axis_index("gy")
    lev = lax.axis_index("lev")
    peer = (g, gx, gy, 1 - lev)
    first = (lev * 2).astype(F32)

    barrier = pltpu.get_barrier_semaphore()
    pl.semaphore_signal(barrier, inc=1, device_id=peer, device_id_type=MESH)
    others = [(i, j) for i in range(gxn) for j in range(gyn) if (i, j) != (0, 0)]
    for i, j in others:
        pl.semaphore_signal(
            barrier,
            inc=1,
            device_id=(g, lax.rem(gx + i, gxn), lax.rem(gy + j, gyn), lev),
            device_id_type=MESH,
        )

    def exists(dr, dc):
        nx, ny = gx + dr, gy + dc
        return (nx >= 0) & (nx < gxn) & (ny >= 0) & (ny < gyn)

    src_rows = {1: (rows - RIM, RIM), 0: (0, rows), -1: (0, RIM)}
    dst_rows = {1: (0, RIM), 0: (RIM, rows), -1: (RIM + rows, RIM)}

    def halo_copy(d):
        dr, dc = MOVES[d]
        s0, n = src_rows[dr]
        t0, _ = dst_rows[dr]
        if dc == 0:
            src = main.at[pl.ds(RIM + s0, n)]
            dst = main.at[pl.ds(t0, n)]
        else:
            src = ecol.at[pl.ds(s0, n)]
            dst = erecv.at[pl.ds(t0, n), pl.ds(0 if dc == 1 else 8, 8)]
        return pltpu.make_async_remote_copy(
            src_ref=src,
            dst_ref=dst,
            send_sem=halo_send.at[d],
            recv_sem=halo_recv.at[d],
            device_id=(g, gx + dr, gy + dc, lev),
            device_id_type=MESH,
        )

    def near_copy(d, src, dst, send, recv):
        dr, dc = MOVES[d]
        return pltpu.make_async_remote_copy(
            src_ref=src,
            dst_ref=dst.at[d],
            send_sem=send.at[d],
            recv_sem=recv.at[d],
            device_id=(g, gx + dr, gy + dc, lev),
            device_id_type=MESH,
        )

    def start_all(copy):
        for d, (dr, dc) in enumerate(MOVES):
            pl.when(exists(dr, dc))(lambda d=d: copy(d).start())

    def recv_all(copy):
        for d, (dr, dc) in enumerate(MOVES):
            pl.when(exists(-dr, -dc))(lambda d=d: copy(d).wait_recv())

    def sent_all(copy):
        for d, (dr, dc) in enumerate(MOVES):
            pl.when(exists(dr, dc))(lambda d=d: copy(d).wait_send())

    obs_copy = lambda d: near_copy(d, opack, orecv, obs_send, obs_recv)
    wt_copy = lambda d: near_copy(d, wown, wrecv, wt_send, wt_recv)

    def lev_copy(k, src, dst):
        return pltpu.make_async_remote_copy(
            src_ref=src,
            dst_ref=dst,
            send_sem=lev_send.at[k],
            recv_sem=lev_recv.at[k],
            device_id=peer,
            device_id_type=MESH,
        )

    c8 = lax.broadcasted_iota(jnp.int32, (8, cols), 0)
    j8 = lax.broadcasted_iota(jnp.int32, (8, cols), 1)
    pick = (j8 == jnp.where(c8 < RIM, c8, cols - 8 + c8)).astype(F32).astype(BF16)
    ecol[...] = jnp.zeros(ecol.shape, F32)

    obs = obs_ref[...]
    level, row_o, col_o, usable = obs[2:3], obs[3:4], obs[4:5], obs[5:6]
    y_sub = lax.broadcasted_iota(jnp.int32, (cols, 128), 0).astype(F32)
    onehot = (y_sub == col_o).astype(F32).astype(BF16)

    acc = jnp.zeros((both, 128), F32)
    for r in range(rows):
        slab = a_in[r]
        main[RIM + r] = slab
        parts = split_three(slab)
        ecol[r, :, 0:both] = sum(dot(pick, p, 1, 1) for p in parts)
        got = sum(dot(p, onehot) for p in parts)
        acc = acc + jnp.where(row_o == float(r), got, 0.0)
    mean = sum(dot(p, onehot) for p in split_three(back_ref[...].reshape(2 * rows, cols)))
    place = lax.broadcasted_iota(jnp.int32, (2 * rows, 128), 0).astype(F32)
    wanted = (level - first) * rows + row_o
    mean = jnp.sum(jnp.where(place == wanted, mean, 0.0), axis=0, keepdims=True)
    mine = jnp.where(level == first, acc[:members], 0.0) + jnp.where(
        level == first + 1.0, acc[members:], 0.0
    )
    opart[0:members] = mine
    opart[members : members + 8] = jnp.broadcast_to(mean, (8, 128))

    for d, (dr, dc) in enumerate(MOVES):
        t0, n = dst_rows[dr]

        @pl.when(jnp.logical_not(exists(-dr, -dc)))
        def _(d=d, dr=dr, dc=dc, t0=t0, n=n):
            if dc == 0:
                main[t0 : t0 + n] = jnp.zeros((n, both, cols), F32)
            else:
                c0 = 0 if dc == 1 else 8
                erecv[t0 : t0 + n, c0 : c0 + 8] = jnp.zeros((n, 8, 128), F32)
            orecv[d] = jnp.zeros(orecv.shape[1:], F32)
            wrecv[d] = jnp.zeros(wrecv.shape[1:], F32)

    pl.semaphore_wait(barrier, gxn * gyn)
    start_all(halo_copy)
    lev_obs = lev_copy(0, opart, opeer)
    lev_obs.start()
    lev_obs.wait_recv()
    full = opart[...] + opeer[...]
    anom_o = full[0:members]
    misfit = obs[0:1] - full[members : members + 1]
    error = obs[1:2]
    spread = jnp.sum(anom_o * anom_o, axis=0, keepdims=True) / (members - 1)
    on = usable > 0.5
    opack[0:members] = anom_o
    opack[members : members + 8] = obs
    start_all(obs_copy)
    stat[...] = jnp.concatenate(
        [
            jnp.where(on, misfit * misfit, 0.0),
            jnp.where(on, spread, 0.0),
            jnp.where(on, error, 0.0),
            jnp.zeros((5, 128), F32),
        ],
        0,
    )

    def stat_copy(k):
        i, j = others[k]
        return pltpu.make_async_remote_copy(
            src_ref=stat,
            dst_ref=srecv.at[k],
            send_sem=st_send.at[k],
            recv_sem=st_recv.at[k],
            device_id=(g, lax.rem(gx + i, gxn), lax.rem(gy + j, gyn), lev),
            device_id_type=MESH,
        )

    for k in range(len(others)):
        stat_copy(k).start()

    recv_all(halo_copy)

    c16 = lax.broadcasted_iota(jnp.int32, (16, cols), 0)
    j16 = lax.broadcasted_iota(jnp.int32, (16, cols), 1)
    put = (
        ((j16 < RIM) & (c16 == j16 + 8)) | ((j16 >= cols - RIM) & (c16 == j16 - (cols - 8)))
    ).astype(F32).astype(BF16)
    wide = 2 * cols
    for e in range(rows + 2 * RIM):
        ext[e, :, 0:cols] = main[e]
        spread_out = sum(dot(p, put, 0, 0) for p in split_three(erecv[e]))
        ext[e, :, cols:wide] = spread_out[0:both]

    extent = rows + 2 * RIM

    def row_sums(e, carry):
        here = ext[e]
        below = ext[jnp.minimum(e + STEP, extent - 1)]
        terms = (
            here * here,
            here * pltpu.roll(below, STEP, 1),
            here * below,
            here * pltpu.roll(below, wide - STEP, 1),
            here * pltpu.roll(here, wide - STEP, 1),
        )
        for k, term in enumerate(terms):
            sums[k, pl.ds(e, 1)] = jnp.sum(term, axis=0, keepdims=True)
        return carry

    lax.fori_loop(0, extent, row_sums, 0)
    lev_sum = lev_copy(1, sums, speer)
    lev_sum.start()
    lev_sum.wait_recv()

    weight_total = float(members * total_levels)
    sq = (sums[0] + speer[0]) / weight_total + EPS
    q0, q1, q2, q3 = [(sums[k] + speer[k]) / weight_total for k in range(1, 5)]
    top = extent - STEP
    s_here, s_below = sq[0:top], sq[STEP:extent]
    g0 = q0[0:top] / jnp.sqrt(s_here * pltpu.roll(s_below, STEP, 1))
    g1 = q1[0:top] / jnp.sqrt(s_here * s_below)
    g2 = q2[0:top] / jnp.sqrt(s_here * pltpu.roll(s_below, wide - STEP, 1))
    g3 = q3[0:top] / jnp.sqrt(s_here * pltpu.roll(s_here, wide - STEP, 1))
    up, dn = slice(0, top - STEP), slice(STEP, top)
    channels = (
        pltpu.roll(g2[up], STEP, 1),
        g1[up],
        pltpu.roll(g0[up], wide - STEP, 1),
        pltpu.roll(g3[dn], STEP, 1),
        g3[dn],
        g0[dn],
        g1[dn],
        g2[dn],
    )
    for k, channel in enumerate(channels):
        feat[:, k, :] = channel

    wts = wts_ref[...]
    w2h, w2l = split_two(wts[:, 0:96])
    w1h, w1l = split_two(wts[:, 96:120])
    w1s, w2s = jnp.concatenate([w1h, w1l], 0), jnp.concatenate([w2h, w2l], 0)
    b1, b2, hw = wts[0:32, 120:121], wts[0:32, 121:122], wts[0:32, 122:123]
    hb = wts[0:1, 123:124]
    lane = lax.broadcasted_iota(jnp.int32, (1, wide), 1)
    col_at = jnp.where(lane < cols + cols // 2, lane, lane - wide) + gy * cols
    col_in = (col_at >= 0) & (col_at < gyn * cols)

    def conv_row(x, wh, ws):
        patch = jnp.concatenate([pltpu.roll(x, 1, 1), x, pltpu.roll(x, wide - 1, 1)], 0)
        high, low = split_two(patch)
        z = dot(ws, high)
        return z[0:96] + z[96:192] + dot(wh, low)

    z1 = [conv_row(feat[i], w1h, w1s) for i in range(3)]
    z2 = []
    tapers = []
    for i in range(rows + 2):
        h = z1[0][0:32] + z1[1][32:64] + z1[2][64:96]
        if i + 3 < rows + 4:
            z1 = [z1[1], z1[2], conv_row(feat[i + 3], w1h, w1s)]
        row_at = gx * rows + (i - 1)
        keep = col_in & (row_at >= 0) & (row_at < gxn * rows)
        h = jnp.where(keep, jnp.maximum(h + b1, 0.0), 0.0)
        z2.append(conv_row(h, w2h, w2s)[:, 0:cols])
        if len(z2) == 3:
            out = z2[0][0:32] + z2[1][32:64] + z2[2][64:96]
            out = jnp.maximum(out + b2, 0.0)
            tapers.append(jnp.sum(out * hw, axis=0, keepdims=True) + hb)
            z2 = z2[1:]
    logits = jnp.concatenate(tapers, 0)
    taper = 1.0 / (1.0 + jnp.exp(-logits))
    taper_ref[...] = taper

    for k in range(len(others)):
        stat_copy(k).wait_recv()
    tot = stat[...]
    for k in range(len(others)):
        tot = tot + srecv[k]
    tot = jnp.sum(tot, axis=1, keepdims=True)
    inflation = tot[0:1] / (tot[1:2] + tot[2:3])
    gain = jnp.where(on, misfit / (inflation * spread + error), 0.0)
    at_obs = sum(dot(p, onehot) for p in split_three(taper))
    place = lax.broadcasted_iota(jnp.int32, (rows, 128), 0).astype(F32)
    at_obs = jnp.sum(jnp.where(place == row_o, at_obs, 0.0), axis=0, keepdims=True)
    weight = at_obs * gain / (members - 1)
    wown[...] = jnp.broadcast_to(weight, (8, 128))
    start_all(wt_copy)
    recv_all(obs_copy)

    tiles = [(tr, tc) for tr in (-1, 0, 1) for tc in (-1, 0, 1)]
    row_list = []
    for t, (tr, tc) in enumerate(tiles):
        pack = opack if (tr, tc) == (0, 0) else orecv.at[MOVES.index((-tr, -tc))]
        gap = y_sub - (pack[members + 4 : members + 5] + float(tc * cols))
        near[:, t * 128 : t * 128 + 128] = gap * gap / float(CUT * CUT)
        row_list.append(pack[members + 3 : members + 4] + float(tr * rows))
    row_all = jnp.concatenate(row_list, 1)
    recv_all(wt_copy)
    for t, (tr, tc) in enumerate(tiles):
        d = None if (tr, tc) == (0, 0) else MOVES.index((-tr, -tc))
        pack = opack if d is None else orecv.at[d]
        w = weight if d is None else wrecv[d, 0:1]
        anom = pack[0:members]
        for l in range(2):
            ratio = (first + float(l) - pack[members + 2 : members + 3]) / VCUT
            vert = jnp.maximum(0.0, 1.0 - ratio * ratio)
            near_coef = (vert * vert * w) * anom
            hid[l * members : (l + 1) * members, t * 128 : t * 128 + 128] = near_coef
    coef[...] = hid[...].astype(BF16)

    for r in range(rows):
        k0 = 0 if r < CUT - 1 else 3 * 128
        k1 = 9 * 128 if r > rows - CUT else 6 * 128
        gap = float(r) - row_all[:, k0:k1]
        base = 1.0 - gap * gap / float(CUT * CUT)
        m = jnp.maximum(0.0, base - near[:, k0:k1])
        local = (m * m).astype(BF16)
        w = dot(coef[:, k0:k1], local, 1, 1)
        prod = main[RIM + r] * w
        scale = inflation * taper[r : r + 1]
        for l in range(2):
            part = jnp.sum(prod[l * members : (l + 1) * members], axis=0, keepdims=True)
            inc_ref[l, r : r + 1] = scale * part

    sent_all(halo_copy)
    sent_all(obs_copy)
    sent_all(wt_copy)
    for k in range(len(others)):
        stat_copy(k).wait_send()
    lev_obs.wait_send()
    lev_sum.wait_send()


def per_device(
    anomaly_codes,
    block_scales,
    background,
    obs_values,
    obs_error,
    obs_cell,
    obs_level,
    obs_count,
    conv1_weight,
    conv1_bias,
    conv2_weight,
    conv2_bias,
    head_weight,
    head_bias,
):
    members, levs, rows, cols = anomaly_codes.shape
    gxn, gyn = lax.axis_size("gx"), lax.axis_size("gy")
    both = members * levs
    a = (anomaly_codes.astype(F32) * block_scales).transpose(2, 1, 0, 3).reshape(rows, both, cols)
    cell = obs_cell[0]
    obs = jnp.concatenate(
        [
            obs_values[0],
            obs_error[0],
            obs_level[0].astype(F32),
            (cell // cols).astype(F32),
            (cell % cols).astype(F32),
            (jnp.arange(128)[None] < obs_count).astype(F32),
            jnp.zeros((2, 128), F32),
        ],
        0,
    )
    w2 = conv2_weight.transpose(0, 3, 1, 2).reshape(96, 96)
    w1 = conv1_weight.transpose(0, 3, 1, 2).reshape(96, 24)
    col = lambda v: jnp.tile(v, 3)[:, None]
    wts = jnp.concatenate(
        [
            w2,
            w1,
            col(conv1_bias),
            col(conv2_bias),
            col(head_weight),
            jnp.broadcast_to(head_bias[None], (96, 1)),
            jnp.zeros((96, 4), F32),
        ],
        1,
    )
    vm = lambda *s, dtype=F32: pltpu.VMEM(s, dtype)
    sem = lambda n: pltpu.SemaphoreType.DMA((n,))
    extent = rows + 2 * RIM
    tiles = gxn * gyn - 1
    return pl.pallas_call(
        functools.partial(kernel, gxn, gyn, members),
        out_shape=(
            jax.ShapeDtypeStruct((levs, rows, cols), F32),
            jax.ShapeDtypeStruct((rows, cols), F32),
        ),
        in_specs=[pl.BlockSpec(memory_space=pltpu.VMEM)] * 4,
        out_specs=[pl.BlockSpec(memory_space=pltpu.VMEM)] * 2,
        scratch_shapes=[
            vm(extent, both, cols),
            vm(extent, both, 2 * cols),
            vm(rows, 8, 128),
            vm(extent, 16, 128),
            vm(members + 8, 128),
            vm(members + 8, 128),
            vm(members + 8, 128),
            vm(8, members + 8, 128),
            vm(5, extent, 2 * cols),
            vm(5, extent, 2 * cols),
            vm(8, 128),
            vm(8, 8, 128),
            vm(8, 128),
            vm(tiles, 8, 128),
            vm(rows + 4, 8, 2 * cols),
            vm(both, 9 * 128),
            vm(cols, 9 * 128),
            vm(both, 9 * 128, dtype=BF16),
            sem(8),
            sem(8),
            sem(8),
            sem(8),
            sem(8),
            sem(8),
            sem(tiles),
            sem(tiles),
            sem(2),
            sem(2),
        ],
        compiler_params=pltpu.CompilerParams(
            collective_id=0, has_side_effects=True, vmem_limit_bytes=40 * 1024 * 1024
        ),
    )(a, background, obs, wts)


def solution(mesh):
    in_specs = (
        P(None, "lev", ("groups", "gx"), "gy"),
        P(None, "lev", ("groups", "gx"), "gy"),
        P("lev", ("groups", "gx"), "gy"),
        P(("groups", "gx"), "gy", None),
        P(("groups", "gx"), "gy", None),
        P(("groups", "gx"), "gy", None),
        P(("groups", "gx"), "gy", None),
        P(("groups", "gx"), "gy"),
        P(),
        P(),
        P(),
        P(),
        P(),
        P(),
    )
    out_specs = (P("lev", ("groups", "gx"), "gy"), P(("groups", "gx"), "gy"))
    return jax.shard_map(
        per_device, mesh=mesh, in_specs=in_specs, out_specs=out_specs, check_vma=False
    )
```

```python
import functools

import jax
import jax.numpy as jnp
from jax import lax
from jax.experimental import pallas as pl
from jax.experimental.pallas import tpu as pltpu
from jax.sharding import PartitionSpec as P

STEP = 2
VCUT = 6
CUT = 6
RIM = 4
EPS = 1e-06
MOVES = ((-1, -1), (-1, 0), (-1, 1), (0, -1), (0, 1), (1, -1), (1, 0), (1, 1))
MESH = pl.DeviceIdType.MESH
F32 = jnp.float32
BF16 = jnp.bfloat16


def split_two(x):
    high = x.astype(BF16)
    return high, (x - high.astype(F32)).astype(BF16)


def split_three(x):
    high = x.astype(BF16)
    rest = x - high.astype(F32)
    middle = rest.astype(BF16)
    return high, middle, (rest - middle.astype(F32)).astype(BF16)


def dot(a, b, ca=1, cb=0):
    return lax.dot_general(a, b, (((ca,), (cb,)), ((), ())), preferred_element_type=F32)


def kernel(
    gxn,
    gyn,
    members,
    codes_ref,
    scale_ref,
    back_ref,
    values_ref,
    error_ref,
    cell_ref,
    level_ref,
    count_ref,
    c1_ref,
    c2_ref,
    b1_ref,
    b2_ref,
    hw_ref,
    hb_ref,
    inc_ref,
    taper_ref,
    main,
    ext,
    ecol,
    erecv,
    opart,
    opeer,
    opack,
    orecv,
    sums,
    speer,
    wown,
    wrecv,
    stat,
    srecv,
    feat,
    hid,
    near,
    coef,
    flat,
    scales,
    wtile,
    local,
    halo_send,
    halo_recv,
    obs_send,
    obs_recv,
    wt_send,
    wt_recv,
    st_send,
    st_recv,
    lev_send,
    lev_recv,
):
    _, levs, rows, cols = codes_ref.shape
    both = members * levs
    total_levels = 2 * 2
    g = lax.axis_index("groups")
    gx = lax.axis_index("gx")
    gy = lax.axis_index("gy")
    lev = lax.axis_index("lev")
    peer = (g, gx, gy, 1 - lev)
    first = (lev * 2).astype(F32)

    barrier = pltpu.get_barrier_semaphore()
    pl.semaphore_signal(barrier, inc=1, device_id=peer, device_id_type=MESH)
    others = [(i, j) for i in range(gxn) for j in range(gyn) if (i, j) != (0, 0)]
    for i, j in others:
        pl.semaphore_signal(
            barrier,
            inc=1,
            device_id=(g, lax.rem(gx + i, gxn), lax.rem(gy + j, gyn), lev),
            device_id_type=MESH,
        )

    def exists(dr, dc):
        nx, ny = gx + dr, gy + dc
        return (nx >= 0) & (nx < gxn) & (ny >= 0) & (ny < gyn)

    src_rows = {1: (rows - RIM, RIM), 0: (0, rows), -1: (0, RIM)}
    dst_rows = {1: (0, RIM), 0: (RIM, rows), -1: (RIM + rows, RIM)}

    def halo_copy(d):
        dr, dc = MOVES[d]
        s0, n = src_rows[dr]
        t0, _ = dst_rows[dr]
        if dc == 0:
            src = main.at[pl.ds(RIM + s0, n)]
            dst = main.at[pl.ds(t0, n)]
        else:
            src = ecol.at[pl.ds(s0, n)]
            dst = erecv.at[pl.ds(t0, n), pl.ds(0 if dc == 1 else 8, 8)]
        return pltpu.make_async_remote_copy(
            src_ref=src,
            dst_ref=dst,
            send_sem=halo_send.at[d],
            recv_sem=halo_recv.at[d],
            device_id=(g, gx + dr, gy + dc, lev),
            device_id_type=MESH,
        )

    def near_copy(d, src, dst, send, recv):
        dr, dc = MOVES[d]
        return pltpu.make_async_remote_copy(
            src_ref=src,
            dst_ref=dst.at[d],
            send_sem=send.at[d],
            recv_sem=recv.at[d],
            device_id=(g, gx + dr, gy + dc, lev),
            device_id_type=MESH,
        )

    def start_all(copy):
        for d, (dr, dc) in enumerate(MOVES):
            pl.when(exists(dr, dc))(lambda d=d: copy(d).start())

    def recv_all(copy):
        for d, (dr, dc) in enumerate(MOVES):
            pl.when(exists(-dr, -dc))(lambda d=d: copy(d).wait_recv())

    def sent_all(copy):
        for d, (dr, dc) in enumerate(MOVES):
            pl.when(exists(dr, dc))(lambda d=d: copy(d).wait_send())

    obs_copy = lambda d: near_copy(d, opack, orecv, obs_send, obs_recv)
    wt_copy = lambda d: near_copy(d, wown, wrecv, wt_send, wt_recv)

    def lev_copy(k, src, dst):
        return pltpu.make_async_remote_copy(
            src_ref=src,
            dst_ref=dst,
            send_sem=lev_send.at[k],
            recv_sem=lev_recv.at[k],
            device_id=peer,
            device_id_type=MESH,
        )

    for l in range(levs):
        for r in range(rows):
            scales[l * rows + r : l * rows + r + 1, 0:members] = scale_ref[l, r]
    flat[...] = codes_ref[...].reshape(both * rows, cols).astype(F32)
    scale_cols = scales[...].T
    spans = [slice(l * members, (l + 1) * members) for l in range(levs)]

    def code_slab(l, r):
        return flat[pl.ds(l * rows + r, members, stride=levs * rows)]

    for r in range(rows):
        for l in range(levs):
            at = l * rows + r
            main[RIM + r, spans[l]] = code_slab(l, r) * scale_cols[0:members, at : at + 1]
    for d, (dr, dc) in enumerate(MOVES):
        t0, n = dst_rows[dr]

        @pl.when(jnp.logical_not(exists(-dr, -dc)))
        def _(d=d, dr=dr, dc=dc, t0=t0, n=n):
            if dc == 0:
                main[t0 : t0 + n] = jnp.zeros((n, both, cols), F32)
            else:
                c0 = 0 if dc == 1 else 8
                erecv[t0 : t0 + n, c0 : c0 + 8] = jnp.zeros((n, 8, 128), F32)
            orecv[d] = jnp.zeros(orecv.shape[1:], F32)
            wrecv[d] = jnp.zeros(wrecv.shape[1:], F32)

    c8 = lax.broadcasted_iota(jnp.int32, (8, cols), 0)
    j8 = lax.broadcasted_iota(jnp.int32, (8, cols), 1)
    pick = (j8 == jnp.where(c8 < RIM, c8, cols - 8 + c8)).astype(F32).astype(BF16)
    ecol[...] = jnp.zeros(ecol.shape, F32)
    for r in range(rows):
        ecol[r, :, 0:both] = sum(dot(pick, p, 1, 1) for p in split_two(main[RIM + r]))

    cell = cell_ref[0]
    level = level_ref[0].astype(F32)
    row_o, col_o = (cell // cols).astype(F32), lax.rem(cell, cols).astype(F32)
    on = lax.broadcasted_iota(jnp.int32, (1, 128), 1) < count_ref[...]
    error = error_ref[0]
    y_sub = lax.broadcasted_iota(jnp.int32, (cols, 128), 0).astype(F32)
    onehot = (y_sub == col_o).astype(F32).astype(BF16)

    pl.semaphore_wait(barrier, gxn * gyn)
    start_all(halo_copy)

    mine = jnp.zeros((members, 128), F32)
    for r in range(rows):
        for l in range(levs):
            at = l * rows + r
            got = dot(code_slab(l, r).astype(BF16), onehot) * scale_cols[0:members, at : at + 1]
            mine = mine + jnp.where((row_o == float(r)) & (level == first + float(l)), got, 0.0)
    mean = sum(dot(p, onehot) for p in split_three(back_ref[...].reshape(2 * rows, cols)))
    place = lax.broadcasted_iota(jnp.int32, (2 * rows, 128), 0).astype(F32)
    wanted = (level - first) * rows + row_o
    mean = jnp.sum(jnp.where(place == wanted, mean, 0.0), axis=0, keepdims=True)
    opart[0:members] = mine
    opart[members : members + 8] = jnp.broadcast_to(mean, (8, 128))

    lev_obs = lev_copy(0, opart, opeer)
    lev_obs.start()
    wtile[...] = jnp.zeros(wtile.shape, F32)
    chans, feats = c2_ref.shape[2], c1_ref.shape[2]
    for i in range(3):
        for j in range(3):
            lanes = slice(i * chans, (i + 1) * chans)
            wtile[j * chans : (j + 1) * chans, lanes] = c2_ref[i, j]
            wtile[96 + j * feats : 96 + (j + 1) * feats, lanes] = c1_ref[i, j]
    wtile[120:121, 0:chans] = b1_ref[...]
    wtile[121:122, 0:chans] = b2_ref[...]
    wtile[122:123, 0:chans] = hw_ref[...]
    wts = wtile[...].T
    w2h, w2l = split_two(wts[0:96, 0:96])
    w1h, w1l = split_two(wts[0:96, 96:120])
    w1s, w2s = jnp.concatenate([w1h, w1l], 0), jnp.concatenate([w2h, w2l], 0)
    b1, b2, hw = wts[0:32, 120:121], wts[0:32, 121:122], wts[0:32, 122:123]
    hb = hb_ref[...]
    wide = 2 * cols
    lane = lax.broadcasted_iota(jnp.int32, (1, wide), 1)
    col_at = jnp.where(lane < cols + cols // 2, lane, lane - wide) + gy * cols
    col_in = (col_at >= 0) & (col_at < gyn * cols)

    lev_obs.wait_recv()
    full = opart[...] + opeer[...]
    anom_o = full[0:members]
    misfit = values_ref[0] - full[members : members + 1]
    spread = jnp.sum(anom_o * anom_o, axis=0, keepdims=True) / (members - 1)
    opack[0:members] = anom_o
    opack[members : members + 8] = jnp.concatenate(
        [level, level, level, row_o, col_o, jnp.zeros((3, 128), F32)], 0
    )
    start_all(obs_copy)
    stat[...] = jnp.concatenate(
        [
            jnp.where(on, misfit * misfit, 0.0),
            jnp.where(on, spread, 0.0),
            jnp.where(on, error, 0.0),
            jnp.zeros((5, 128), F32),
        ],
        0,
    )

    def stat_copy(k):
        i, j = others[k]
        return pltpu.make_async_remote_copy(
            src_ref=stat,
            dst_ref=srecv.at[k],
            send_sem=st_send.at[k],
            recv_sem=st_recv.at[k],
            device_id=(g, lax.rem(gx + i, gxn), lax.rem(gy + j, gyn), lev),
            device_id_type=MESH,
        )

    for k in range(len(others)):
        stat_copy(k).start()

    recv_all(halo_copy)

    c16 = lax.broadcasted_iota(jnp.int32, (16, cols), 0)
    j16 = lax.broadcasted_iota(jnp.int32, (16, cols), 1)
    put = (
        ((j16 < RIM) & (c16 == j16 + 8)) | ((j16 >= cols - RIM) & (c16 == j16 - (cols - 8)))
    ).astype(F32).astype(BF16)
    for e in range(rows + 2 * RIM):
        ext[e, :, 0:cols] = main[e]
        spread_out = sum(dot(p, put, 0, 0) for p in split_two(erecv[e]))
        ext[e, :, cols:wide] = spread_out[0:both]

    extent = rows + 2 * RIM

    def row_sums(e, carry):
        here = ext[e]
        below = ext[jnp.minimum(e + STEP, extent - 1)]
        terms = (
            here * here,
            here * pltpu.roll(below, STEP, 1),
            here * below,
            here * pltpu.roll(below, wide - STEP, 1),
            here * pltpu.roll(here, wide - STEP, 1),
        )
        for k, term in enumerate(terms):
            sums[k, pl.ds(e, 1)] = jnp.sum(term, axis=0, keepdims=True)
        return carry

    lax.fori_loop(0, extent, row_sums, 0)
    lev_sum = lev_copy(1, sums, speer)
    lev_sum.start()
    lev_sum.wait_recv()

    weight_total = float(members * total_levels)
    sq = (sums[0] + speer[0]) / weight_total + EPS
    q0, q1, q2, q3 = [(sums[k] + speer[k]) / weight_total for k in range(1, 5)]
    top = extent - STEP
    s_here, s_below = sq[0:top], sq[STEP:extent]
    g0 = q0[0:top] / jnp.sqrt(s_here * pltpu.roll(s_below, STEP, 1))
    g1 = q1[0:top] / jnp.sqrt(s_here * s_below)
    g2 = q2[0:top] / jnp.sqrt(s_here * pltpu.roll(s_below, wide - STEP, 1))
    g3 = q3[0:top] / jnp.sqrt(s_here * pltpu.roll(s_here, wide - STEP, 1))
    up, dn = slice(0, top - STEP), slice(STEP, top)
    channels = (
        pltpu.roll(g2[up], STEP, 1),
        g1[up],
        pltpu.roll(g0[up], wide - STEP, 1),
        pltpu.roll(g3[dn], STEP, 1),
        g3[dn],
        g0[dn],
        g1[dn],
        g2[dn],
    )
    for k, channel in enumerate(channels):
        feat[:, k, :] = channel

    def conv_row(x, wh, ws):
        patch = jnp.concatenate([pltpu.roll(x, 1, 1), x, pltpu.roll(x, wide - 1, 1)], 0)
        high, low = split_two(patch)
        z = dot(ws, high)
        return z[0:96] + z[96:192] + dot(wh, low)

    z1 = [conv_row(feat[i], w1h, w1s) for i in range(3)]
    z2 = []
    tapers = []
    for i in range(rows + 2):
        h = z1[0][0:32] + z1[1][32:64] + z1[2][64:96]
        if i + 3 < rows + 4:
            z1 = [z1[1], z1[2], conv_row(feat[i + 3], w1h, w1s)]
        row_at = gx * rows + (i - 1)
        keep = col_in & (row_at >= 0) & (row_at < gxn * rows)
        h = jnp.where(keep, jnp.maximum(h + b1, 0.0), 0.0)
        z2.append(conv_row(h, w2h, w2s)[:, 0:cols])
        if len(z2) == 3:
            out = z2[0][0:32] + z2[1][32:64] + z2[2][64:96]
            out = jnp.maximum(out + b2, 0.0)
            tapers.append(jnp.sum(out * hw, axis=0, keepdims=True) + hb)
            z2 = z2[1:]
    logits = jnp.concatenate(tapers, 0)
    taper = 1.0 / (1.0 + jnp.exp(-logits))
    taper_ref[...] = taper

    for k in range(len(others)):
        stat_copy(k).wait_recv()
    tot = stat[...]
    for k in range(len(others)):
        tot = tot + srecv[k]
    tot = jnp.sum(tot, axis=1, keepdims=True)
    inflation = tot[0:1] / (tot[1:2] + tot[2:3])
    gain = jnp.where(on, misfit / (inflation * spread + error), 0.0)
    at_obs = sum(dot(p, onehot) for p in split_three(taper))
    place = lax.broadcasted_iota(jnp.int32, (rows, 128), 0).astype(F32)
    at_obs = jnp.sum(jnp.where(place == row_o, at_obs, 0.0), axis=0, keepdims=True)
    weight = at_obs * gain / (members - 1)
    wown[...] = jnp.broadcast_to(weight, (8, 128))
    start_all(wt_copy)
    recv_all(obs_copy)

    tiles = [(tr, tc) for tr in (-1, 0, 1) for tc in (-1, 0, 1)]
    row_list = []
    for t, (tr, tc) in enumerate(tiles):
        pack = opack if (tr, tc) == (0, 0) else orecv.at[MOVES.index((-tr, -tc))]
        gap = y_sub - (pack[members + 4 : members + 5] + float(tc * cols))
        near[:, t * 128 : t * 128 + 128] = gap * gap / float(CUT * CUT)
        row_list.append(pack[members + 3 : members + 4] + float(tr * rows))
    row_all = jnp.concatenate(row_list, 1)

    def near_span(r):
        return (0 if r < CUT - 1 else 3 * 128), (9 * 128 if r > rows - CUT else 6 * 128)

    for r in range(rows):
        k0, k1 = near_span(r)
        gap = float(r) - row_all[:, k0:k1]
        base = 1.0 - gap * gap / float(CUT * CUT)
        m = jnp.maximum(0.0, base - near[:, k0:k1])
        local[r, :, 0 : k1 - k0] = (m * m).astype(BF16)
    recv_all(wt_copy)
    for t, (tr, tc) in enumerate(tiles):
        d = None if (tr, tc) == (0, 0) else MOVES.index((-tr, -tc))
        pack = opack if d is None else orecv.at[d]
        w = weight if d is None else wrecv[d, 0:1]
        anom = pack[0:members]
        for l in range(2):
            ratio = (first + float(l) - pack[members + 2 : members + 3]) / VCUT
            vert = jnp.maximum(0.0, 1.0 - ratio * ratio)
            near_coef = (vert * vert * w) * anom
            hid[l * members : (l + 1) * members, t * 128 : t * 128 + 128] = near_coef
    coef[...] = hid[...].astype(BF16)

    for r in range(rows):
        k0, k1 = near_span(r)
        w = dot(coef[:, k0:k1], local[r, :, 0 : k1 - k0], 1, 1)
        prod = main[RIM + r] * w
        scale = inflation * taper[r : r + 1]
        for l in range(2):
            part = jnp.sum(prod[l * members : (l + 1) * members], axis=0, keepdims=True)
            inc_ref[l, r : r + 1] = scale * part

    sent_all(halo_copy)
    sent_all(obs_copy)
    sent_all(wt_copy)
    for k in range(len(others)):
        stat_copy(k).wait_send()
    lev_obs.wait_send()
    lev_sum.wait_send()


def per_device(
    anomaly_codes,
    block_scales,
    background,
    obs_values,
    obs_error,
    obs_cell,
    obs_level,
    obs_count,
    conv1_weight,
    conv1_bias,
    conv2_weight,
    conv2_bias,
    head_weight,
    head_bias,
):
    members, levs, rows, cols = anomaly_codes.shape
    gxn, gyn = lax.axis_size("gx"), lax.axis_size("gy")
    both = members * levs
    scales = block_scales.transpose(1, 2, 3, 0)
    row = lambda v: v.reshape(1, -1)
    vm = lambda *s, dtype=F32: pltpu.VMEM(s, dtype)
    sem = lambda n: pltpu.SemaphoreType.DMA((n,))
    extent = rows + 2 * RIM
    tiles = gxn * gyn - 1
    return pl.pallas_call(
        functools.partial(kernel, gxn, gyn, members),
        out_shape=(
            jax.ShapeDtypeStruct((levs, rows, cols), F32),
            jax.ShapeDtypeStruct((rows, cols), F32),
        ),
        in_specs=[pl.BlockSpec(memory_space=pltpu.VMEM)] * 14,
        out_specs=[pl.BlockSpec(memory_space=pltpu.VMEM)] * 2,
        scratch_shapes=[
            vm(extent, both, cols),
            vm(extent, both, 2 * cols),
            vm(rows, 8, 128),
            vm(extent, 16, 128),
            vm(members + 8, 128),
            vm(members + 8, 128),
            vm(members + 8, 128),
            vm(8, members + 8, 128),
            vm(5, extent, 2 * cols),
            vm(5, extent, 2 * cols),
            vm(8, 128),
            vm(8, 8, 128),
            vm(8, 128),
            vm(tiles, 8, 128),
            vm(rows + 4, 8, 2 * cols),
            vm(both, 9 * 128),
            vm(cols, 9 * 128),
            vm(both, 9 * 128, dtype=BF16),
            vm(both * rows, cols),
            vm(128, 128),
            vm(128, 128),
            vm(rows, cols, 6 * 128, dtype=BF16),
            sem(8),
            sem(8),
            sem(8),
            sem(8),
            sem(8),
            sem(8),
            sem(tiles),
            sem(tiles),
            sem(2),
            sem(2),
        ],
        compiler_params=pltpu.CompilerParams(
            collective_id=0, has_side_effects=True, vmem_limit_bytes=40 * 1024 * 1024
        ),
    )(
        anomaly_codes,
        scales,
        background,
        obs_values,
        obs_error,
        obs_cell,
        obs_level,
        obs_count,
        conv1_weight,
        conv2_weight,
        row(conv1_bias),
        row(conv2_bias),
        row(head_weight),
        row(head_bias),
    )


def solution(mesh):
    in_specs = (
        P(None, "lev", ("groups", "gx"), "gy"),
        P(None, "lev", ("groups", "gx"), "gy"),
        P("lev", ("groups", "gx"), "gy"),
        P(("groups", "gx"), "gy", None),
        P(("groups", "gx"), "gy", None),
        P(("groups", "gx"), "gy", None),
        P(("groups", "gx"), "gy", None),
        P(("groups", "gx"), "gy"),
        P(),
        P(),
        P(),
        P(),
        P(),
        P(),
    )
    out_specs = (P("lev", ("groups", "gx"), "gy"), P(("groups", "gx"), "gy"))
    return jax.shard_map(
        per_device, mesh=mesh, in_specs=in_specs, out_specs=out_specs, check_vma=False
    )
```

```python
import functools

import jax
import jax.numpy as jnp
from jax import lax
from jax.experimental import pallas as pl
from jax.experimental.pallas import tpu as pltpu
from jax.sharding import PartitionSpec as P

STEP = 2
VCUT = 6
CUT = 6
RIM = 4
EPS = 1e-06
MOVES = ((-1, -1), (-1, 0), (-1, 1), (0, -1), (0, 1), (1, -1), (1, 0), (1, 1))
MESH = pl.DeviceIdType.MESH
F32 = jnp.float32
BF16 = jnp.bfloat16


def split_two(x):
    high = x.astype(BF16)
    return high, (x - high.astype(F32)).astype(BF16)


def split_three(x):
    high = x.astype(BF16)
    rest = x - high.astype(F32)
    middle = rest.astype(BF16)
    return high, middle, (rest - middle.astype(F32)).astype(BF16)


def dot(a, b, ca=1, cb=0):
    return lax.dot_general(a, b, (((ca,), (cb,)), ((), ())), preferred_element_type=F32)


def kernel(
    gxn,
    gyn,
    members,
    codes_hbm,
    scale_hbm,
    back_hbm,
    values_hbm,
    error_hbm,
    cell_hbm,
    level_hbm,
    count_hbm,
    c1_hbm,
    c2_hbm,
    b1_hbm,
    b2_hbm,
    hw_hbm,
    hb_hbm,
    inc_ref,
    taper_ref,
    main,
    ext,
    ecol,
    erecv,
    opart,
    opeer,
    opack,
    orecv,
    sums,
    speer,
    wown,
    wrecv,
    stat,
    srecv,
    feat,
    hid,
    coef,
    flat,
    scales,
    wtile,
    local,
    rolled,
    codes_ref,
    scale_ref,
    back_ref,
    values_ref,
    error_ref,
    cell_ref,
    level_ref,
    count_ref,
    c1_ref,
    c2_ref,
    b1_ref,
    b2_ref,
    hw_ref,
    hb_ref,
    in_sem,
    halo_send,
    halo_recv,
    obs_send,
    obs_recv,
    wt_send,
    wt_recv,
    st_send,
    st_recv,
    lev_send,
    lev_recv,
):
    _, levs, rows, cols = codes_ref.shape
    both = members * levs
    total_levels = 2 * 2
    g = lax.axis_index("groups")
    gx = lax.axis_index("gx")
    gy = lax.axis_index("gy")
    lev = lax.axis_index("lev")
    peer = (g, gx, gy, 1 - lev)
    first = (lev * 2).astype(F32)

    hbm = (codes_hbm, scale_hbm, back_hbm, values_hbm, error_hbm, cell_hbm, level_hbm, count_hbm, c1_hbm, c2_hbm, b1_hbm, b2_hbm, hw_hbm, hb_hbm)
    held = (codes_ref, scale_ref, back_ref, values_ref, error_ref, cell_ref, level_ref, count_ref, c1_ref, c2_ref, b1_ref, b2_ref, hw_ref, hb_ref)
    fetch = [pltpu.make_async_copy(x, v, in_sem.at[k]) for k, (x, v) in enumerate(zip(hbm, held))]
    for copy in fetch:
        copy.start()
    barrier = pltpu.get_barrier_semaphore()
    pl.semaphore_signal(barrier, inc=1, device_id=peer, device_id_type=MESH)
    others = [(i, j) for i in range(gxn) for j in range(gyn) if (i, j) != (0, 0)]
    for i, j in others:
        pl.semaphore_signal(
            barrier,
            inc=1,
            device_id=(g, lax.rem(gx + i, gxn), lax.rem(gy + j, gyn), lev),
            device_id_type=MESH,
        )

    def exists(dr, dc):
        nx, ny = gx + dr, gy + dc
        return (nx >= 0) & (nx < gxn) & (ny >= 0) & (ny < gyn)

    src_rows = {1: (rows - RIM, RIM), 0: (0, rows), -1: (0, RIM)}
    dst_rows = {1: (0, RIM), 0: (RIM, rows), -1: (RIM + rows, RIM)}

    def halo_copy(d):
        dr, dc = MOVES[d]
        s0, n = src_rows[dr]
        t0, _ = dst_rows[dr]
        if dc == 0:
            src = main.at[pl.ds(RIM + s0, n)]
            dst = main.at[pl.ds(t0, n)]
        else:
            src = ecol.at[pl.ds(s0, n)]
            dst = erecv.at[pl.ds(t0, n), pl.ds(0 if dc == 1 else 8, 8)]
        return pltpu.make_async_remote_copy(
            src_ref=src,
            dst_ref=dst,
            send_sem=halo_send.at[d],
            recv_sem=halo_recv.at[d],
            device_id=(g, gx + dr, gy + dc, lev),
            device_id_type=MESH,
        )

    def near_copy(d, src, dst, send, recv):
        dr, dc = MOVES[d]
        return pltpu.make_async_remote_copy(
            src_ref=src,
            dst_ref=dst.at[d],
            send_sem=send.at[d],
            recv_sem=recv.at[d],
            device_id=(g, gx + dr, gy + dc, lev),
            device_id_type=MESH,
        )

    def start_all(copy):
        for d, (dr, dc) in enumerate(MOVES):
            pl.when(exists(dr, dc))(lambda d=d: copy(d).start())

    def recv_all(copy):
        for d, (dr, dc) in enumerate(MOVES):
            pl.when(exists(-dr, -dc))(lambda d=d: copy(d).wait_recv())

    def sent_all(copy):
        for d, (dr, dc) in enumerate(MOVES):
            pl.when(exists(dr, dc))(lambda d=d: copy(d).wait_send())

    obs_copy = lambda d: near_copy(d, opack, orecv, obs_send, obs_recv)
    wt_copy = lambda d: near_copy(d, wown, wrecv, wt_send, wt_recv)

    def lev_copy(k, src, dst):
        return pltpu.make_async_remote_copy(
            src_ref=src,
            dst_ref=dst,
            send_sem=lev_send.at[k],
            recv_sem=lev_recv.at[k],
            device_id=peer,
            device_id_type=MESH,
        )

    for copy in fetch:
        copy.wait()
    for l in range(levs):
        for r in range(rows):
            scales[l * rows + r : l * rows + r + 1, 0:members] = scale_ref[l, r]
    flat[...] = codes_ref[...].reshape(both * rows, cols).astype(F32)
    scale_cols = scales[...].T
    spans = [slice(l * members, (l + 1) * members) for l in range(levs)]

    def code_slab(l, r):
        return flat[pl.ds(l * rows + r, members, stride=levs * rows)]

    for r in range(rows):
        for l in range(levs):
            at = l * rows + r
            main[RIM + r, spans[l]] = code_slab(l, r) * scale_cols[0:members, at : at + 1]
    for d, (dr, dc) in enumerate(MOVES):
        t0, n = dst_rows[dr]

        @pl.when(jnp.logical_not(exists(-dr, -dc)))
        def _(d=d, dr=dr, dc=dc, t0=t0, n=n):
            if dc == 0:
                main[t0 : t0 + n] = jnp.zeros((n, both, cols), F32)
            else:
                c0 = 0 if dc == 1 else 8
                erecv[t0 : t0 + n, c0 : c0 + 8] = jnp.zeros((n, 8, 128), F32)
            orecv[d] = jnp.zeros(orecv.shape[1:], F32)
            wrecv[d] = jnp.zeros(wrecv.shape[1:], F32)

    c8 = lax.broadcasted_iota(jnp.int32, (8, cols), 0)
    j8 = lax.broadcasted_iota(jnp.int32, (8, cols), 1)
    pick = (j8 == jnp.where(c8 < RIM, c8, cols - 8 + c8)).astype(F32).astype(BF16)
    ecol[...] = jnp.zeros(ecol.shape, F32)
    for r in range(rows):
        ecol[r, :, 0:both] = sum(dot(pick, p, 1, 1) for p in split_two(main[RIM + r]))

    cell = cell_ref[0]
    level = level_ref[0].astype(F32)
    row_o, col_o = (cell // cols).astype(F32), lax.rem(cell, cols).astype(F32)
    on = lax.broadcasted_iota(jnp.int32, (1, 128), 1) < count_ref[...]
    error = error_ref[0]
    y_sub = lax.broadcasted_iota(jnp.int32, (cols, 128), 0).astype(F32)
    onehot = (y_sub == col_o).astype(F32).astype(BF16)

    pl.semaphore_wait(barrier, gxn * gyn)
    start_all(halo_copy)

    mine = jnp.zeros((members, 128), F32)
    for r in range(rows):
        for l in range(levs):
            at = l * rows + r
            got = dot(code_slab(l, r).astype(BF16), onehot) * scale_cols[0:members, at : at + 1]
            mine = mine + jnp.where((row_o == float(r)) & (level == first + float(l)), got, 0.0)
    mean = sum(dot(p, onehot) for p in split_three(back_ref[...].reshape(2 * rows, cols)))
    place = lax.broadcasted_iota(jnp.int32, (2 * rows, 128), 0).astype(F32)
    wanted = (level - first) * rows + row_o
    mean = jnp.sum(jnp.where(place == wanted, mean, 0.0), axis=0, keepdims=True)
    opart[0:members] = mine
    opart[members : members + 8] = jnp.broadcast_to(mean, (8, 128))

    lev_obs = lev_copy(0, opart, opeer)
    lev_obs.start()
    wtile[...] = jnp.zeros(wtile.shape, F32)
    chans, feats = c2_ref.shape[2], c1_ref.shape[2]
    for i in range(3):
        for j in range(3):
            lanes = slice(i * chans, (i + 1) * chans)
            wtile[j * chans : (j + 1) * chans, lanes] = c2_ref[i, j]
            wtile[96 + j * feats : 96 + (j + 1) * feats, lanes] = c1_ref[i, j]
    wtile[120:121, 0:chans] = b1_ref[...]
    wtile[121:122, 0:chans] = b2_ref[...]
    wtile[122:123, 0:chans] = hw_ref[...]
    wts = wtile[...].T
    w2h, w2l = split_two(wts[0:96, 0:96])
    w1h, w1l = split_two(wts[0:96, 96:120])
    w1s, w2s = jnp.concatenate([w1h, w1l], 0), jnp.concatenate([w2h, w2l], 0)
    b1, b2, hw = wts[0:32, 120:121], wts[0:32, 121:122], wts[0:32, 122:123]
    hb = hb_ref[...]
    wide = 2 * cols
    lane = lax.broadcasted_iota(jnp.int32, (1, wide), 1)
    col_at = jnp.where(lane < cols + cols // 2, lane, lane - wide) + gy * cols
    col_in = (col_at >= 0) & (col_at < gyn * cols)

    lev_obs.wait_recv()
    full = opart[...] + opeer[...]
    anom_o = full[0:members]
    misfit = values_ref[0] - full[members : members + 1]
    spread = jnp.sum(anom_o * anom_o, axis=0, keepdims=True) / (members - 1)
    opack[0:members] = anom_o
    opack[members : members + 8] = jnp.concatenate(
        [level, level, level, row_o, col_o, jnp.zeros((3, 128), F32)], 0
    )
    start_all(obs_copy)
    stat[...] = jnp.concatenate(
        [
            jnp.where(on, misfit * misfit, 0.0),
            jnp.where(on, spread, 0.0),
            jnp.where(on, error, 0.0),
            jnp.zeros((5, 128), F32),
        ],
        0,
    )

    def stat_copy(k):
        i, j = others[k]
        return pltpu.make_async_remote_copy(
            src_ref=stat,
            dst_ref=srecv.at[k],
            send_sem=st_send.at[k],
            recv_sem=st_recv.at[k],
            device_id=(g, lax.rem(gx + i, gxn), lax.rem(gy + j, gyn), lev),
            device_id_type=MESH,
        )

    for k in range(len(others)):
        stat_copy(k).start()

    recv_all(halo_copy)

    c16 = lax.broadcasted_iota(jnp.int32, (16, cols), 0)
    j16 = lax.broadcasted_iota(jnp.int32, (16, cols), 1)
    put = (
        ((j16 < RIM) & (c16 == j16 + 8)) | ((j16 >= cols - RIM) & (c16 == j16 - (cols - 8)))
    ).astype(F32).astype(BF16)
    for e in range(rows + 2 * RIM):
        ext[e, :, 0:cols] = main[e]
        spread_out = sum(dot(p, put, 0, 0) for p in split_two(erecv[e]))
        ext[e, :, cols:wide] = spread_out[0:both]
        rolled[e] = pltpu.roll(ext[e], wide - STEP, 1)

    extent = rows + 2 * RIM

    for e in range(extent):
        here, here_next = ext[e], rolled[e]
        terms = [here * here]
        if e < extent - STEP:
            below, below_next = ext[e + STEP], rolled[e + STEP]
            terms += [here_next * below, here * below, here * below_next]
        else:
            terms += [jnp.zeros_like(here[0:8])] * 3
        terms.append(here * here_next)
        for k, term in enumerate(terms):
            sums[k, e : e + 1] = jnp.sum(term, axis=0, keepdims=True)
    lev_sum = lev_copy(1, sums, speer)
    lev_sum.start()
    lev_sum.wait_recv()

    weight_total = float(members * total_levels)
    sq = (sums[0] + speer[0]) / weight_total + EPS
    q0, q1, q2, q3 = [(sums[k] + speer[k]) / weight_total for k in range(1, 5)]
    q0 = pltpu.roll(q0, STEP, 1)
    top = extent - STEP
    s_here, s_below = sq[0:top], sq[STEP:extent]
    g0 = q0[0:top] / jnp.sqrt(s_here * pltpu.roll(s_below, STEP, 1))
    g1 = q1[0:top] / jnp.sqrt(s_here * s_below)
    g2 = q2[0:top] / jnp.sqrt(s_here * pltpu.roll(s_below, wide - STEP, 1))
    g3 = q3[0:top] / jnp.sqrt(s_here * pltpu.roll(s_here, wide - STEP, 1))
    up, dn = slice(0, top - STEP), slice(STEP, top)
    channels = (
        pltpu.roll(g2[up], STEP, 1),
        g1[up],
        pltpu.roll(g0[up], wide - STEP, 1),
        pltpu.roll(g3[dn], STEP, 1),
        g3[dn],
        g0[dn],
        g1[dn],
        g2[dn],
    )
    for k, channel in enumerate(channels):
        feat[:, k, :] = channel

    def conv_row(x, wh, ws, lanes):
        patch = jnp.concatenate([pltpu.roll(x, 1, 1), x, pltpu.roll(x, wide - 1, 1)], 0)
        high, low = split_two(patch[:, 0:lanes])
        z = dot(ws, high)
        return z[0:96] + z[96:192] + dot(wh, low)

    z1 = [conv_row(feat[i], w1h, w1s, wide) for i in range(3)]
    z2 = []
    tapers = []
    for i in range(rows + 2):
        h = z1[0][0:32] + z1[1][32:64] + z1[2][64:96]
        if i + 3 < rows + 4:
            z1 = [z1[1], z1[2], conv_row(feat[i + 3], w1h, w1s, wide)]
        row_at = gx * rows + (i - 1)
        keep = col_in & (row_at >= 0) & (row_at < gxn * rows)
        h = jnp.where(keep, jnp.maximum(h + b1, 0.0), 0.0)
        z2.append(conv_row(h, w2h, w2s, cols))
        if len(z2) == 3:
            out = z2[0][0:32] + z2[1][32:64] + z2[2][64:96]
            out = jnp.maximum(out + b2, 0.0)
            tapers.append(jnp.sum(out * hw, axis=0, keepdims=True) + hb)
            z2 = z2[1:]
    logits = jnp.concatenate(tapers, 0)
    taper = 1.0 / (1.0 + jnp.exp(-logits))
    taper_ref[...] = taper

    for k in range(len(others)):
        stat_copy(k).wait_recv()
    tot = stat[...]
    for k in range(len(others)):
        tot = tot + srecv[k]
    tot = jnp.sum(tot, axis=1, keepdims=True)
    inflation = tot[0:1] / (tot[1:2] + tot[2:3])
    gain = jnp.where(on, misfit / (inflation * spread + error), 0.0)
    at_obs = sum(dot(p, onehot) for p in split_three(taper))
    place = lax.broadcasted_iota(jnp.int32, (rows, 128), 0).astype(F32)
    at_obs = jnp.sum(jnp.where(place == row_o, at_obs, 0.0), axis=0, keepdims=True)
    weight = at_obs * gain / (members - 1)
    wown[...] = jnp.broadcast_to(weight, (8, 128))
    start_all(wt_copy)
    recv_all(obs_copy)

    tiles = [(tr, tc) for tr in (-1, 0, 1) for tc in (-1, 0, 1)]
    def near_span(r):
        return (0 if r < CUT - 1 else 3 * 128), (9 * 128 if r > rows - CUT else 6 * 128)

    lanes = lax.broadcasted_iota(jnp.int32, (128, cols), 1).astype(F32)
    for t, (tr, tc) in enumerate(tiles):
        pack = opack if (tr, tc) == (0, 0) else orecv.at[MOVES.index((-tr, -tc))]
        spots = pack[members : members + 8].T
        gap = lanes - (spots[:, 4:5] + float(tc * cols))
        near = gap * gap / float(CUT * CUT)
        gap = lanes - (spots[:, 3:4] + float(tr * rows))
        base = 1.0 - gap * gap / float(CUT * CUT)
        for r in range(rows):
            if (tr == -1 and r >= CUT - 1) or (tr == 1 and r <= rows - CUT):
                continue
            m = jnp.maximum(0.0, base[:, r : r + 1] - near)
            k0 = t * 128 - near_span(r)[0]
            local[r, k0 : k0 + 128] = (m * m).astype(BF16)
    recv_all(wt_copy)
    for t, (tr, tc) in enumerate(tiles):
        d = None if (tr, tc) == (0, 0) else MOVES.index((-tr, -tc))
        pack = opack if d is None else orecv.at[d]
        w = weight if d is None else wrecv[d, 0:1]
        anom = pack[0:members]
        for l in range(2):
            ratio = (first + float(l) - pack[members + 2 : members + 3]) / VCUT
            vert = jnp.maximum(0.0, 1.0 - ratio * ratio)
            near_coef = (vert * vert * w) * anom
            hid[l * members : (l + 1) * members, t * 128 : t * 128 + 128] = near_coef
    coef[...] = hid[...].astype(BF16)

    for r in range(rows):
        k0, k1 = near_span(r)
        w = dot(coef[:, k0:k1], local[r, 0 : k1 - k0])
        prod = main[RIM + r] * w
        scale = inflation * taper[r : r + 1]
        for l in range(2):
            part = jnp.sum(prod[l * members : (l + 1) * members], axis=0, keepdims=True)
            inc_ref[l, r : r + 1] = scale * part

    sent_all(halo_copy)
    sent_all(obs_copy)
    sent_all(wt_copy)
    for k in range(len(others)):
        stat_copy(k).wait_send()
    lev_obs.wait_send()
    lev_sum.wait_send()


def per_device(
    anomaly_codes,
    block_scales,
    background,
    obs_values,
    obs_error,
    obs_cell,
    obs_level,
    obs_count,
    conv1_weight,
    conv1_bias,
    conv2_weight,
    conv2_bias,
    head_weight,
    head_bias,
):
    members, levs, rows, cols = anomaly_codes.shape
    gxn, gyn = lax.axis_size("gx"), lax.axis_size("gy")
    both = members * levs
    scales = block_scales.transpose(1, 2, 3, 0)
    row = lambda v: v.reshape(1, -1)
    args = (
        anomaly_codes,
        scales,
        background,
        obs_values,
        obs_error,
        obs_cell,
        obs_level,
        obs_count,
        conv1_weight,
        conv2_weight,
        row(conv1_bias),
        row(conv2_bias),
        row(head_weight),
        row(head_bias),
    )
    vm = lambda *s, dtype=F32: pltpu.VMEM(s, dtype)
    sem = lambda n: pltpu.SemaphoreType.DMA((n,))
    extent = rows + 2 * RIM
    tiles = gxn * gyn - 1
    return pl.pallas_call(
        functools.partial(kernel, gxn, gyn, members),
        out_shape=(
            jax.ShapeDtypeStruct((levs, rows, cols), F32),
            jax.ShapeDtypeStruct((rows, cols), F32),
        ),
        in_specs=[pl.BlockSpec(memory_space=pltpu.HBM)] * len(args),
        out_specs=[pl.BlockSpec(memory_space=pltpu.VMEM)] * 2,
        scratch_shapes=[
            vm(extent, both, cols),
            vm(extent, both, 2 * cols),
            vm(rows, 8, 128),
            vm(extent, 16, 128),
            vm(members + 8, 128),
            vm(members + 8, 128),
            vm(members + 8, 128),
            vm(8, members + 8, 128),
            vm(5, extent, 2 * cols),
            vm(5, extent, 2 * cols),
            vm(8, 128),
            vm(8, 8, 128),
            vm(8, 128),
            vm(tiles, 8, 128),
            vm(rows + 4, 8, 2 * cols),
            vm(both, 9 * 128),
            vm(both, 9 * 128, dtype=BF16),
            vm(both * rows, cols),
            vm(128, 128),
            vm(128, 128),
            vm(rows, 6 * 128, cols, dtype=BF16),
            vm(extent, both, 2 * cols),
            *[vm(*x.shape, dtype=x.dtype) for x in args],
            sem(len(args)),
            sem(8),
            sem(8),
            sem(8),
            sem(8),
            sem(8),
            sem(8),
            sem(tiles),
            sem(tiles),
            sem(2),
            sem(2),
        ],
        compiler_params=pltpu.CompilerParams(
            collective_id=0, has_side_effects=True, vmem_limit_bytes=62 * 1024 * 1024
        ),
    )(*args)


def solution(mesh):
    in_specs = (
        P(None, "lev", ("groups", "gx"), "gy"),
        P(None, "lev", ("groups", "gx"), "gy"),
        P("lev", ("groups", "gx"), "gy"),
        P(("groups", "gx"), "gy", None),
        P(("groups", "gx"), "gy", None),
        P(("groups", "gx"), "gy", None),
        P(("groups", "gx"), "gy", None),
        P(("groups", "gx"), "gy"),
        P(),
        P(),
        P(),
        P(),
        P(),
        P(),
    )
    out_specs = (P("lev", ("groups", "gx"), "gy"), P(("groups", "gx"), "gy"))
    return jax.shard_map(
        per_device, mesh=mesh, in_specs=in_specs, out_specs=out_specs, check_vma=False
    )
```

```python
import functools

import jax
import jax.numpy as jnp
from jax import lax
from jax.experimental import pallas as pl
from jax.experimental.pallas import tpu as pltpu
from jax.sharding import PartitionSpec as P

STEP = 2
VCUT = 6
CUT = 6
RIM = 4
EPS = 1e-06
MOVES = ((-1, -1), (-1, 0), (-1, 1), (0, -1), (0, 1), (1, -1), (1, 0), (1, 1))
MESH = pl.DeviceIdType.MESH
F32 = jnp.float32
BF16 = jnp.bfloat16


def split_two(x):
    high = x.astype(BF16)
    return high, (x - high.astype(F32)).astype(BF16)


def split_three(x):
    high = x.astype(BF16)
    rest = x - high.astype(F32)
    middle = rest.astype(BF16)
    return high, middle, (rest - middle.astype(F32)).astype(BF16)


def dot(a, b, ca=1, cb=0):
    return lax.dot_general(a, b, (((ca,), (cb,)), ((), ())), preferred_element_type=F32)


def kernel(
    gxn,
    gyn,
    members,
    codes_hbm,
    scale_hbm,
    back_hbm,
    values_hbm,
    error_hbm,
    cell_hbm,
    level_hbm,
    count_hbm,
    c1_hbm,
    c2_hbm,
    b1_hbm,
    b2_hbm,
    hw_hbm,
    hb_hbm,
    inc_ref,
    taper_ref,
    main,
    ext,
    ecol,
    erecv,
    opart,
    opeer,
    opack,
    orecv,
    sums,
    speer,
    wown,
    wrecv,
    stat,
    srecv,
    feat,
    hid,
    coef,
    flat,
    scales,
    wtile,
    local,
    rolled,
    codes_ref,
    scale_ref,
    back_ref,
    values_ref,
    error_ref,
    cell_ref,
    level_ref,
    count_ref,
    c1_ref,
    c2_ref,
    b1_ref,
    b2_ref,
    hw_ref,
    hb_ref,
    in_sem,
    halo_send,
    halo_recv,
    obs_send,
    obs_recv,
    wt_send,
    wt_recv,
    st_send,
    st_recv,
    lev_send,
    lev_recv,
):
    _, levs, rows, cols = codes_ref.shape
    both = members * levs
    total_levels = 2 * 2
    g = lax.axis_index("groups")
    gx = lax.axis_index("gx")
    gy = lax.axis_index("gy")
    lev = lax.axis_index("lev")
    peer = (g, gx, gy, 1 - lev)
    first = (lev * 2).astype(F32)

    hbm = (codes_hbm, scale_hbm, back_hbm, values_hbm, error_hbm, cell_hbm, level_hbm, count_hbm, c1_hbm, c2_hbm, b1_hbm, b2_hbm, hw_hbm, hb_hbm)
    held = (codes_ref, scale_ref, back_ref, values_ref, error_ref, cell_ref, level_ref, count_ref, c1_ref, c2_ref, b1_ref, b2_ref, hw_ref, hb_ref)
    fetch = [pltpu.make_async_copy(x, v, in_sem.at[k]) for k, (x, v) in enumerate(zip(hbm, held))]
    for copy in fetch:
        copy.start()
    barrier = pltpu.get_barrier_semaphore()
    pl.semaphore_signal(barrier, inc=1, device_id=peer, device_id_type=MESH)
    others = [(i, j) for i in range(gxn) for j in range(gyn) if (i, j) != (0, 0)]
    for i, j in others:
        pl.semaphore_signal(
            barrier,
            inc=1,
            device_id=(g, lax.rem(gx + i, gxn), lax.rem(gy + j, gyn), lev),
            device_id_type=MESH,
        )

    def exists(dr, dc):
        nx, ny = gx + dr, gy + dc
        return (nx >= 0) & (nx < gxn) & (ny >= 0) & (ny < gyn)

    src_rows = {1: (rows - RIM, RIM), 0: (0, rows), -1: (0, RIM)}
    dst_rows = {1: (0, RIM), 0: (RIM, rows), -1: (RIM + rows, RIM)}

    def halo_copy(d):
        dr, dc = MOVES[d]
        s0, n = src_rows[dr]
        t0, _ = dst_rows[dr]
        if dc == 0:
            src = main.at[pl.ds(RIM + s0, n)]
            dst = main.at[pl.ds(t0, n)]
        else:
            src = ecol.at[pl.ds(s0, n)]
            dst = erecv.at[pl.ds(t0, n), pl.ds(0 if dc == 1 else 8, 8)]
        return pltpu.make_async_remote_copy(
            src_ref=src,
            dst_ref=dst,
            send_sem=halo_send.at[d],
            recv_sem=halo_recv.at[d],
            device_id=(g, gx + dr, gy + dc, lev),
            device_id_type=MESH,
        )

    def near_copy(d, src, dst, send, recv):
        dr, dc = MOVES[d]
        return pltpu.make_async_remote_copy(
            src_ref=src,
            dst_ref=dst.at[d],
            send_sem=send.at[d],
            recv_sem=recv.at[d],
            device_id=(g, gx + dr, gy + dc, lev),
            device_id_type=MESH,
        )

    def start_all(copy, moves=range(8)):
        for d in moves:
            dr, dc = MOVES[d]
            pl.when(exists(dr, dc))(lambda d=d: copy(d).start())

    def recv_all(copy, moves=range(8)):
        for d in moves:
            dr, dc = MOVES[d]
            pl.when(exists(-dr, -dc))(lambda d=d: copy(d).wait_recv())

    def sent_all(copy):
        for d, (dr, dc) in enumerate(MOVES):
            pl.when(exists(dr, dc))(lambda d=d: copy(d).wait_send())

    obs_copy = lambda d: near_copy(d, opack, orecv, obs_send, obs_recv)
    wt_copy = lambda d: near_copy(d, wown, wrecv, wt_send, wt_recv)

    def lev_copy(k, src, dst):
        return pltpu.make_async_remote_copy(
            src_ref=src,
            dst_ref=dst,
            send_sem=lev_send.at[k],
            recv_sem=lev_recv.at[k],
            device_id=peer,
            device_id_type=MESH,
        )

    for copy in fetch:
        copy.wait()
    for l in range(levs):
        for r in range(rows):
            scales[l * rows + r : l * rows + r + 1, 0:members] = scale_ref[l, r]
    flat[...] = codes_ref[...].reshape(both * rows, cols).astype(F32)
    scale_cols = scales[...].T
    spans = [slice(l * members, (l + 1) * members) for l in range(levs)]

    def code_slab(l, r):
        return flat[pl.ds(l * rows + r, members, stride=levs * rows)]

    for r in range(rows):
        for l in range(levs):
            at = l * rows + r
            main[RIM + r, spans[l]] = code_slab(l, r) * scale_cols[0:members, at : at + 1]
    for d, (dr, dc) in enumerate(MOVES):
        t0, n = dst_rows[dr]

        @pl.when(jnp.logical_not(exists(-dr, -dc)))
        def _(d=d, dr=dr, dc=dc, t0=t0, n=n):
            if dc == 0:
                main[t0 : t0 + n] = jnp.zeros((n, both, cols), F32)
            else:
                c0 = 0 if dc == 1 else 8
                erecv[t0 : t0 + n, c0 : c0 + 8] = jnp.zeros((n, 8, 128), F32)
            orecv[d] = jnp.zeros(orecv.shape[1:], F32)
            wrecv[d] = jnp.zeros(wrecv.shape[1:], F32)

    pl.semaphore_wait(barrier, gxn * gyn)
    start_all(halo_copy, (1, 6))

    c8 = lax.broadcasted_iota(jnp.int32, (8, cols), 0)
    j8 = lax.broadcasted_iota(jnp.int32, (8, cols), 1)
    pick = (j8 == jnp.where(c8 < RIM, c8, cols - 8 + c8)).astype(F32).astype(BF16)
    ecol[...] = jnp.zeros(ecol.shape, F32)
    for r in range(rows):
        ecol[r, :, 0:both] = sum(dot(pick, p, 1, 1) for p in split_two(main[RIM + r]))
    start_all(halo_copy, (3, 4, 0, 2, 5, 7))

    cell = cell_ref[0]
    level = level_ref[0].astype(F32)
    row_o, col_o = (cell // cols).astype(F32), lax.rem(cell, cols).astype(F32)
    on = lax.broadcasted_iota(jnp.int32, (1, 128), 1) < count_ref[...]
    error = error_ref[0]
    y_sub = lax.broadcasted_iota(jnp.int32, (cols, 128), 0).astype(F32)
    onehot = (y_sub == col_o).astype(F32).astype(BF16)

    mine = jnp.zeros((members, 128), F32)
    for r in range(rows):
        for l in range(levs):
            at = l * rows + r
            got = dot(code_slab(l, r).astype(BF16), onehot) * scale_cols[0:members, at : at + 1]
            mine = mine + jnp.where((row_o == float(r)) & (level == first + float(l)), got, 0.0)
    mean = sum(dot(p, onehot) for p in split_three(back_ref[...].reshape(2 * rows, cols)))
    place = lax.broadcasted_iota(jnp.int32, (2 * rows, 128), 0).astype(F32)
    wanted = (level - first) * rows + row_o
    mean = jnp.sum(jnp.where(place == wanted, mean, 0.0), axis=0, keepdims=True)
    opart[0:members] = mine
    opart[members : members + 8] = jnp.broadcast_to(mean, (8, 128))

    lev_obs = lev_copy(0, opart, opeer)
    lev_obs.start()
    wtile[...] = jnp.zeros(wtile.shape, F32)
    chans, feats = c2_ref.shape[2], c1_ref.shape[2]
    for i in range(3):
        for j in range(3):
            lanes = slice(i * chans, (i + 1) * chans)
            wtile[j * chans : (j + 1) * chans, lanes] = c2_ref[i, j]
            wtile[96 + j * feats : 96 + (j + 1) * feats, lanes] = c1_ref[i, j]
    wtile[120:121, 0:chans] = b1_ref[...]
    wtile[121:122, 0:chans] = b2_ref[...]
    wtile[122:123, 0:chans] = hw_ref[...]
    wts = wtile[...].T
    w2h, w2l = split_two(wts[0:96, 0:96])
    w1h, w1l = split_two(wts[0:96, 96:120])
    w1s, w2s = jnp.concatenate([w1h, w1l], 0), jnp.concatenate([w2h, w2l], 0)
    b1, b2, hw = wts[0:32, 120:121], wts[0:32, 121:122], wts[0:32, 122:123]
    hb = hb_ref[...]
    wide = 2 * cols
    lane = lax.broadcasted_iota(jnp.int32, (1, wide), 1)
    col_at = jnp.where(lane < cols + cols // 2, lane, lane - wide) + gy * cols
    col_in = (col_at >= 0) & (col_at < gyn * cols)

    lev_obs.wait_recv()
    full = opart[...] + opeer[...]
    anom_o = full[0:members]
    misfit = values_ref[0] - full[members : members + 1]
    spread = jnp.sum(anom_o * anom_o, axis=0, keepdims=True) / (members - 1)
    opack[0:members] = anom_o
    opack[members : members + 8] = jnp.concatenate(
        [level, level, level, row_o, col_o, jnp.zeros((3, 128), F32)], 0
    )
    start_all(obs_copy)
    stat[...] = jnp.concatenate(
        [
            jnp.where(on, misfit * misfit, 0.0),
            jnp.where(on, spread, 0.0),
            jnp.where(on, error, 0.0),
            jnp.zeros((5, 128), F32),
        ],
        0,
    )

    def stat_copy(k):
        i, j = others[k]
        return pltpu.make_async_remote_copy(
            src_ref=stat,
            dst_ref=srecv.at[k],
            send_sem=st_send.at[k],
            recv_sem=st_recv.at[k],
            device_id=(g, lax.rem(gx + i, gxn), lax.rem(gy + j, gyn), lev),
            device_id_type=MESH,
        )

    for k in range(len(others)):
        stat_copy(k).start()

    recv_all(halo_copy, (3, 4))

    c16 = lax.broadcasted_iota(jnp.int32, (16, cols), 0)
    j16 = lax.broadcasted_iota(jnp.int32, (16, cols), 1)
    put = (
        ((j16 < RIM) & (c16 == j16 + 8)) | ((j16 >= cols - RIM) & (c16 == j16 - (cols - 8)))
    ).astype(F32).astype(BF16)
    extent = rows + 2 * RIM

    def widen(e):
        ext[e, :, 0:cols] = main[e]
        spread_out = sum(dot(p, put, 0, 0) for p in split_two(erecv[e]))
        ext[e, :, cols:wide] = spread_out[0:both]
        rolled[e] = pltpu.roll(ext[e], wide - STEP, 1)

    def row_sums(e):
        here, here_next = ext[e], rolled[e]
        terms = [here * here]
        if e < extent - STEP:
            below, below_next = ext[e + STEP], rolled[e + STEP]
            terms += [here_next * below, here * below, here * below_next]
        else:
            terms += [jnp.zeros_like(here[0:8])] * 3
        terms.append(here * here_next)
        for k, term in enumerate(terms):
            sums[k, e : e + 1] = jnp.sum(term, axis=0, keepdims=True)

    inner = list(range(RIM, RIM + rows))
    for e in inner:
        widen(e)
    for e in inner[:-STEP]:
        row_sums(e)
    recv_all(halo_copy, (0, 1, 2, 5, 6, 7))
    rim = [e for e in range(extent) if e not in inner]
    for e in rim:
        widen(e)
    for e in rim + inner[-STEP:]:
        row_sums(e)
    lev_sum = lev_copy(1, sums, speer)
    lev_sum.start()
    lev_sum.wait_recv()

    weight_total = float(members * total_levels)
    sq = (sums[0] + speer[0]) / weight_total + EPS
    q0, q1, q2, q3 = [(sums[k] + speer[k]) / weight_total for k in range(1, 5)]
    q0 = pltpu.roll(q0, STEP, 1)
    top = extent - STEP
    s_here, s_below = sq[0:top], sq[STEP:extent]
    g0 = q0[0:top] / jnp.sqrt(s_here * pltpu.roll(s_below, STEP, 1))
    g1 = q1[0:top] / jnp.sqrt(s_here * s_below)
    g2 = q2[0:top] / jnp.sqrt(s_here * pltpu.roll(s_below, wide - STEP, 1))
    g3 = q3[0:top] / jnp.sqrt(s_here * pltpu.roll(s_here, wide - STEP, 1))
    up, dn = slice(0, top - STEP), slice(STEP, top)
    channels = (
        pltpu.roll(g2[up], STEP, 1),
        g1[up],
        pltpu.roll(g0[up], wide - STEP, 1),
        pltpu.roll(g3[dn], STEP, 1),
        g3[dn],
        g0[dn],
        g1[dn],
        g2[dn],
    )
    for k, channel in enumerate(channels):
        feat[:, k, :] = channel

    def conv_row(x, wh, ws, lanes):
        patch = jnp.concatenate([pltpu.roll(x, 1, 1), x, pltpu.roll(x, wide - 1, 1)], 0)
        high, low = split_two(patch[:, 0:lanes])
        z = dot(ws, high)
        return z[0:96] + z[96:192] + dot(wh, low)

    z1 = [conv_row(feat[i], w1h, w1s, wide) for i in range(3)]
    z2 = []
    tapers = []
    for i in range(rows + 2):
        h = z1[0][0:32] + z1[1][32:64] + z1[2][64:96]
        if i + 3 < rows + 4:
            z1 = [z1[1], z1[2], conv_row(feat[i + 3], w1h, w1s, wide)]
        row_at = gx * rows + (i - 1)
        keep = col_in & (row_at >= 0) & (row_at < gxn * rows)
        h = jnp.where(keep, jnp.maximum(h + b1, 0.0), 0.0)
        z2.append(conv_row(h, w2h, w2s, cols))
        if len(z2) == 3:
            out = z2[0][0:32] + z2[1][32:64] + z2[2][64:96]
            out = jnp.maximum(out + b2, 0.0)
            tapers.append(jnp.sum(out * hw, axis=0, keepdims=True) + hb)
            z2 = z2[1:]
    logits = jnp.concatenate(tapers, 0)
    taper = 1.0 / (1.0 + jnp.exp(-logits))
    taper_ref[...] = taper

    for k in range(len(others)):
        stat_copy(k).wait_recv()
    tot = stat[...]
    for k in range(len(others)):
        tot = tot + srecv[k]
    tot = jnp.sum(tot, axis=1, keepdims=True)
    inflation = tot[0:1] / (tot[1:2] + tot[2:3])
    gain = jnp.where(on, misfit / (inflation * spread + error), 0.0)
    at_obs = sum(dot(p, onehot) for p in split_three(taper))
    place = lax.broadcasted_iota(jnp.int32, (rows, 128), 0).astype(F32)
    at_obs = jnp.sum(jnp.where(place == row_o, at_obs, 0.0), axis=0, keepdims=True)
    weight = at_obs * gain / (members - 1)
    wown[...] = jnp.broadcast_to(weight, (8, 128))
    start_all(wt_copy)
    recv_all(obs_copy)

    tiles = [(tr, tc) for tr in (-1, 0, 1) for tc in (-1, 0, 1)]
    def near_span(r):
        return (0 if r < CUT - 1 else 3 * 128), (9 * 128 if r > rows - CUT else 6 * 128)

    lanes = lax.broadcasted_iota(jnp.int32, (128, cols), 1).astype(F32)
    for t, (tr, tc) in enumerate(tiles):
        pack = opack if (tr, tc) == (0, 0) else orecv.at[MOVES.index((-tr, -tc))]
        spots = pack[members : members + 8].T
        gap = lanes - (spots[:, 4:5] + float(tc * cols))
        near = gap * gap / float(CUT * CUT)
        gap = lanes - (spots[:, 3:4] + float(tr * rows))
        base = 1.0 - gap * gap / float(CUT * CUT)
        for r in range(rows):
            if (tr == -1 and r >= CUT - 1) or (tr == 1 and r <= rows - CUT):
                continue
            m = jnp.maximum(0.0, base[:, r : r + 1] - near)
            k0 = t * 128 - near_span(r)[0]
            local[r, k0 : k0 + 128] = (m * m).astype(BF16)
    recv_all(wt_copy)
    for t, (tr, tc) in enumerate(tiles):
        d = None if (tr, tc) == (0, 0) else MOVES.index((-tr, -tc))
        pack = opack if d is None else orecv.at[d]
        w = weight if d is None else wrecv[d, 0:1]
        anom = pack[0:members]
        for l in range(2):
            ratio = (first + float(l) - pack[members + 2 : members + 3]) / VCUT
            vert = jnp.maximum(0.0, 1.0 - ratio * ratio)
            near_coef = (vert * vert * w) * anom
            hid[l * members : (l + 1) * members, t * 128 : t * 128 + 128] = near_coef
    coef[...] = hid[...].astype(BF16)

    for r in range(rows):
        k0, k1 = near_span(r)
        w = dot(coef[:, k0:k1], local[r, 0 : k1 - k0])
        prod = main[RIM + r] * w
        scale = inflation * taper[r : r + 1]
        for l in range(2):
            part = jnp.sum(prod[l * members : (l + 1) * members], axis=0, keepdims=True)
            inc_ref[l * rows + r : l * rows + r + 1] = scale * part

    sent_all(halo_copy)
    sent_all(obs_copy)
    sent_all(wt_copy)
    for k in range(len(others)):
        stat_copy(k).wait_send()
    lev_obs.wait_send()
    lev_sum.wait_send()


def per_device(
    anomaly_codes,
    block_scales,
    background,
    obs_values,
    obs_error,
    obs_cell,
    obs_level,
    obs_count,
    conv1_weight,
    conv1_bias,
    conv2_weight,
    conv2_bias,
    head_weight,
    head_bias,
):
    members, levs, rows, cols = anomaly_codes.shape
    gxn, gyn = lax.axis_size("gx"), lax.axis_size("gy")
    both = members * levs
    scales = block_scales.transpose(1, 2, 3, 0)
    row = lambda v: v.reshape(1, -1)
    args = (
        anomaly_codes,
        scales,
        background,
        obs_values,
        obs_error,
        obs_cell,
        obs_level,
        obs_count,
        conv1_weight,
        conv2_weight,
        row(conv1_bias),
        row(conv2_bias),
        row(head_weight),
        row(head_bias),
    )
    vm = lambda *s, dtype=F32: pltpu.VMEM(s, dtype)
    sem = lambda n: pltpu.SemaphoreType.DMA((n,))
    extent = rows + 2 * RIM
    tiles = gxn * gyn - 1
    inc, taper = pl.pallas_call(
        functools.partial(kernel, gxn, gyn, members),
        out_shape=(
            jax.ShapeDtypeStruct((levs * rows, cols), F32),
            jax.ShapeDtypeStruct((rows, cols), F32),
        ),
        in_specs=[pl.BlockSpec(memory_space=pltpu.HBM)] * len(args),
        out_specs=[pl.BlockSpec(memory_space=pltpu.VMEM)] * 2,
        scratch_shapes=[
            vm(extent, both, cols),
            vm(extent, both, 2 * cols),
            vm(rows, 8, 128),
            vm(extent, 16, 128),
            vm(members + 8, 128),
            vm(members + 8, 128),
            vm(members + 8, 128),
            vm(8, members + 8, 128),
            vm(5, extent, 2 * cols),
            vm(5, extent, 2 * cols),
            vm(8, 128),
            vm(8, 8, 128),
            vm(8, 128),
            vm(tiles, 8, 128),
            vm(rows + 4, 8, 2 * cols),
            vm(both, 9 * 128),
            vm(both, 9 * 128, dtype=BF16),
            vm(both * rows, cols),
            vm(128, 128),
            vm(128, 128),
            vm(rows, 6 * 128, cols, dtype=BF16),
            vm(extent, both, 2 * cols),
            *[vm(*x.shape, dtype=x.dtype) for x in args],
            sem(len(args)),
            sem(8),
            sem(8),
            sem(8),
            sem(8),
            sem(8),
            sem(8),
            sem(tiles),
            sem(tiles),
            sem(2),
            sem(2),
        ],
        compiler_params=pltpu.CompilerParams(
            collective_id=0, has_side_effects=True, vmem_limit_bytes=62 * 1024 * 1024
        ),
    )(*args)
    return inc.reshape(levs, rows, cols), taper


def solution(mesh):
    in_specs = (
        P(None, "lev", ("groups", "gx"), "gy"),
        P(None, "lev", ("groups", "gx"), "gy"),
        P("lev", ("groups", "gx"), "gy"),
        P(("groups", "gx"), "gy", None),
        P(("groups", "gx"), "gy", None),
        P(("groups", "gx"), "gy", None),
        P(("groups", "gx"), "gy", None),
        P(("groups", "gx"), "gy"),
        P(),
        P(),
        P(),
        P(),
        P(),
        P(),
    )
    out_specs = (P("lev", ("groups", "gx"), "gy"), P(("groups", "gx"), "gy"))
    return jax.shard_map(
        per_device, mesh=mesh, in_specs=in_specs, out_specs=out_specs, check_vma=False
    )
```

```python
import functools

import jax
import jax.numpy as jnp
from jax import lax
from jax.experimental import pallas as pl
from jax.experimental.pallas import tpu as pltpu
from jax.sharding import PartitionSpec as P

STEP = 2
VCUT = 6
CUT = 6
RIM = 4
EPS = 1e-06
MOVES = ((-1, -1), (-1, 0), (-1, 1), (0, -1), (0, 1), (1, -1), (1, 0), (1, 1))
MESH = pl.DeviceIdType.MESH
F32 = jnp.float32
BF16 = jnp.bfloat16


def split_two(x):
    high = x.astype(BF16)
    return high, (x - high.astype(F32)).astype(BF16)


def split_three(x):
    high = x.astype(BF16)
    rest = x - high.astype(F32)
    middle = rest.astype(BF16)
    return high, middle, (rest - middle.astype(F32)).astype(BF16)


def dot(a, b, ca=1, cb=0):
    return lax.dot_general(a, b, (((ca,), (cb,)), ((), ())), preferred_element_type=F32)


def kernel(
    gxn,
    gyn,
    members,
    codes_hbm,
    scale_hbm,
    back_hbm,
    values_hbm,
    error_hbm,
    cell_hbm,
    level_hbm,
    count_hbm,
    c1_hbm,
    c2_hbm,
    b1_hbm,
    b2_hbm,
    hw_hbm,
    hb_hbm,
    inc_ref,
    taper_ref,
    main,
    ext,
    ecol,
    erecv,
    opart,
    opeer,
    opack,
    orecv,
    sums,
    speer,
    wown,
    wrecv,
    stat,
    srecv,
    feat,
    hid,
    coef,
    flat,
    scales,
    wtile,
    local,
    rolled,
    codes_ref,
    scale_ref,
    back_ref,
    values_ref,
    error_ref,
    cell_ref,
    level_ref,
    count_ref,
    c1_ref,
    c2_ref,
    b1_ref,
    b2_ref,
    hw_ref,
    hb_ref,
    in_sem,
    halo_send,
    halo_recv,
    obs_send,
    obs_recv,
    wt_send,
    wt_recv,
    st_send,
    st_recv,
    lev_send,
    lev_recv,
):
    _, levs, rows, cols = codes_ref.shape
    both = members * levs
    total_levels = 2 * 2
    g = lax.axis_index("groups")
    gx = lax.axis_index("gx")
    gy = lax.axis_index("gy")
    lev = lax.axis_index("lev")
    peer = (g, gx, gy, 1 - lev)
    first = (lev * 2).astype(F32)

    hbm = (codes_hbm, scale_hbm, back_hbm, values_hbm, error_hbm, cell_hbm, level_hbm, count_hbm, c1_hbm, c2_hbm, b1_hbm, b2_hbm, hw_hbm, hb_hbm)
    held = (codes_ref, scale_ref, back_ref, values_ref, error_ref, cell_ref, level_ref, count_ref, c1_ref, c2_ref, b1_ref, b2_ref, hw_ref, hb_ref)
    fetch = [pltpu.make_async_copy(x, v, in_sem.at[k]) for k, (x, v) in enumerate(zip(hbm, held))]
    for copy in fetch:
        copy.start()
    barrier = pltpu.get_barrier_semaphore()
    pl.semaphore_signal(barrier, inc=1, device_id=peer, device_id_type=MESH)
    others = [(i, j) for i in range(gxn) for j in range(gyn) if (i, j) != (0, 0)]
    for i, j in others:
        pl.semaphore_signal(
            barrier,
            inc=1,
            device_id=(g, lax.rem(gx + i, gxn), lax.rem(gy + j, gyn), lev),
            device_id_type=MESH,
        )

    def exists(dr, dc):
        nx, ny = gx + dr, gy + dc
        return (nx >= 0) & (nx < gxn) & (ny >= 0) & (ny < gyn)

    src_rows = {1: (rows - RIM, RIM), 0: (0, rows), -1: (0, RIM)}
    dst_rows = {1: (0, RIM), 0: (RIM, rows), -1: (RIM + rows, RIM)}

    def halo_copy(d):
        dr, dc = MOVES[d]
        s0, n = src_rows[dr]
        t0, _ = dst_rows[dr]
        if dc == 0:
            src = main.at[pl.ds(RIM + s0, n)]
            dst = main.at[pl.ds(t0, n)]
        else:
            src = ecol.at[pl.ds(s0, n)]
            dst = erecv.at[pl.ds(t0, n), pl.ds(0 if dc == 1 else 8, 8)]
        return pltpu.make_async_remote_copy(
            src_ref=src,
            dst_ref=dst,
            send_sem=halo_send.at[d],
            recv_sem=halo_recv.at[d],
            device_id=(g, gx + dr, gy + dc, lev),
            device_id_type=MESH,
        )

    def near_copy(d, src, dst, send, recv):
        dr, dc = MOVES[d]
        return pltpu.make_async_remote_copy(
            src_ref=src,
            dst_ref=dst.at[d],
            send_sem=send.at[d],
            recv_sem=recv.at[d],
            device_id=(g, gx + dr, gy + dc, lev),
            device_id_type=MESH,
        )

    def start_all(copy, moves=range(8)):
        for d in moves:
            dr, dc = MOVES[d]
            pl.when(exists(dr, dc))(lambda d=d: copy(d).start())

    def recv_all(copy, moves=range(8)):
        for d in moves:
            dr, dc = MOVES[d]
            pl.when(exists(-dr, -dc))(lambda d=d: copy(d).wait_recv())

    def sent_all(copy):
        for d, (dr, dc) in enumerate(MOVES):
            pl.when(exists(dr, dc))(lambda d=d: copy(d).wait_send())

    obs_copy = lambda d: near_copy(d, opack, orecv, obs_send, obs_recv)
    wt_copy = lambda d: near_copy(d, wown, wrecv, wt_send, wt_recv)

    def lev_copy(k, src, dst):
        return pltpu.make_async_remote_copy(
            src_ref=src,
            dst_ref=dst,
            send_sem=lev_send.at[k],
            recv_sem=lev_recv.at[k],
            device_id=peer,
            device_id_type=MESH,
        )

    for copy in fetch:
        copy.wait()
    for l in range(levs):
        for r in range(rows):
            scales[l * rows + r : l * rows + r + 1, 0:members] = scale_ref[l, r]
    flat[...] = codes_ref[...].reshape(both * rows, cols).astype(F32)
    scale_cols = scales[...].T
    spans = [slice(l * members, (l + 1) * members) for l in range(levs)]

    def code_slab(l, r):
        return flat[pl.ds(l * rows + r, members, stride=levs * rows)]

    for r in range(rows):
        for l in range(levs):
            at = l * rows + r
            main[RIM + r, spans[l]] = code_slab(l, r) * scale_cols[0:members, at : at + 1]
    for d, (dr, dc) in enumerate(MOVES):
        t0, n = dst_rows[dr]

        @pl.when(jnp.logical_not(exists(-dr, -dc)))
        def _(d=d, dr=dr, dc=dc, t0=t0, n=n):
            if dc == 0:
                main[t0 : t0 + n] = jnp.zeros((n, both, cols), F32)
            else:
                c0 = 0 if dc == 1 else 8
                erecv[t0 : t0 + n, c0 : c0 + 8] = jnp.zeros((n, 8, 128), F32)
            orecv[d] = jnp.zeros(orecv.shape[1:], F32)
            wrecv[d] = jnp.zeros(wrecv.shape[1:], F32)

    pl.semaphore_wait(barrier, gxn * gyn)
    start_all(halo_copy, (1, 6))

    c8 = lax.broadcasted_iota(jnp.int32, (8, cols), 0)
    j8 = lax.broadcasted_iota(jnp.int32, (8, cols), 1)
    pick = (j8 == jnp.where(c8 < RIM, c8, cols - 8 + c8)).astype(F32).astype(BF16)
    ecol[...] = jnp.zeros(ecol.shape, F32)
    for r in range(rows):
        ecol[r, :, 0:both] = sum(dot(pick, p, 1, 1) for p in split_two(main[RIM + r]))
    start_all(halo_copy, (3, 4, 0, 2, 5, 7))

    cell = cell_ref[0]
    level = level_ref[0].astype(F32)
    row_o, col_o = (cell // cols).astype(F32), lax.rem(cell, cols).astype(F32)
    on = lax.broadcasted_iota(jnp.int32, (1, 128), 1) < count_ref[...]
    error = error_ref[0]
    y_sub = lax.broadcasted_iota(jnp.int32, (cols, 128), 0).astype(F32)
    onehot = (y_sub == col_o).astype(F32).astype(BF16)

    mine = jnp.zeros((members, 128), F32)
    for r in range(rows):
        for l in range(levs):
            at = l * rows + r
            got = dot(code_slab(l, r).astype(BF16), onehot) * scale_cols[0:members, at : at + 1]
            mine = mine + jnp.where((row_o == float(r)) & (level == first + float(l)), got, 0.0)
    mean = sum(dot(p, onehot) for p in split_three(back_ref[...].reshape(2 * rows, cols)))
    place = lax.broadcasted_iota(jnp.int32, (2 * rows, 128), 0).astype(F32)
    wanted = (level - first) * rows + row_o
    mean = jnp.sum(jnp.where(place == wanted, mean, 0.0), axis=0, keepdims=True)
    opart[0:members] = mine
    opart[members : members + 8] = jnp.broadcast_to(mean, (8, 128))

    lev_obs = lev_copy(0, opart, opeer)
    lev_obs.start()
    wtile[...] = jnp.zeros(wtile.shape, F32)
    chans, feats = c2_ref.shape[2], c1_ref.shape[2]
    for i in range(3):
        for j in range(3):
            lanes = slice(i * chans, (i + 1) * chans)
            wtile[j * chans : (j + 1) * chans, lanes] = c2_ref[i, j]
            wtile[96 + j * feats : 96 + (j + 1) * feats, lanes] = c1_ref[i, j]
    wtile[120:121, 0:chans] = b1_ref[...]
    wtile[121:122, 0:chans] = b2_ref[...]
    wtile[122:123, 0:chans] = hw_ref[...]
    wts = wtile[...].T
    w2h, w2l = split_two(wts[0:96, 0:96])
    w1h, w1l = split_two(wts[0:96, 96:120])
    w1s, w2s = jnp.concatenate([w1h, w1l], 0), jnp.concatenate([w2h, w2l], 0)
    b1, b2, hw = wts[0:32, 120:121], wts[0:32, 121:122], wts[0:32, 122:123]
    hb = hb_ref[...]
    wide = 2 * cols
    lane = lax.broadcasted_iota(jnp.int32, (1, wide), 1)
    col_at = jnp.where(lane < cols + cols // 2, lane, lane - wide) + gy * cols
    col_in = (col_at >= 0) & (col_at < gyn * cols)

    lev_obs.wait_recv()
    full = opart[...] + opeer[...]
    anom_o = full[0:members]
    misfit = values_ref[0] - full[members : members + 1]
    spread = jnp.sum(anom_o * anom_o, axis=0, keepdims=True) / (members - 1)
    opack[0:members] = anom_o
    opack[members : members + 8] = jnp.concatenate(
        [level, level, level, row_o, col_o, jnp.zeros((3, 128), F32)], 0
    )
    start_all(obs_copy)
    stat[...] = jnp.concatenate(
        [
            jnp.where(on, misfit * misfit, 0.0),
            jnp.where(on, spread, 0.0),
            jnp.where(on, error, 0.0),
            jnp.zeros((5, 128), F32),
        ],
        0,
    )

    def stat_copy(k):
        i, j = others[k]
        return pltpu.make_async_remote_copy(
            src_ref=stat,
            dst_ref=srecv.at[k],
            send_sem=st_send.at[k],
            recv_sem=st_recv.at[k],
            device_id=(g, lax.rem(gx + i, gxn), lax.rem(gy + j, gyn), lev),
            device_id_type=MESH,
        )

    for k in range(len(others)):
        stat_copy(k).start()

    recv_all(halo_copy, (3, 4))

    c16 = lax.broadcasted_iota(jnp.int32, (16, cols), 0)
    j16 = lax.broadcasted_iota(jnp.int32, (16, cols), 1)
    put = (
        ((j16 < RIM) & (c16 == j16 + 8)) | ((j16 >= cols - RIM) & (c16 == j16 - (cols - 8)))
    ).astype(F32).astype(BF16)
    extent = rows + 2 * RIM

    def widen(e):
        ext[e, :, 0:cols] = main[e]
        spread_out = sum(dot(p, put, 0, 0) for p in split_two(erecv[e]))
        ext[e, :, cols:wide] = spread_out[0:both]
        rolled[e] = pltpu.roll(ext[e], wide - STEP, 1)

    def row_sums(e):
        here, here_next = ext[e], rolled[e]
        terms = [here * here]
        if e < extent - STEP:
            below, below_next = ext[e + STEP], rolled[e + STEP]
            terms += [here_next * below, here * below, here * below_next]
        else:
            terms += [jnp.zeros_like(here[0:8])] * 3
        terms.append(here * here_next)
        for k, term in enumerate(terms):
            sums[k, e : e + 1] = jnp.sum(term, axis=0, keepdims=True)

    inner = list(range(RIM, RIM + rows))
    for e in inner:
        widen(e)
    for e in inner[:-STEP]:
        row_sums(e)
    recv_all(halo_copy, (0, 1, 2, 5, 6, 7))
    rim = [e for e in range(extent) if e not in inner]
    for e in rim:
        widen(e)
    for e in rim + inner[-STEP:]:
        row_sums(e)
    lev_sum = lev_copy(1, sums, speer)
    lev_sum.start()
    recv_all(obs_copy)

    tiles = [(tr, tc) for tr in (-1, 0, 1) for tc in (-1, 0, 1)]
    def near_span(r):
        return (0 if r < CUT - 1 else 3 * 128), (9 * 128 if r > rows - CUT else 6 * 128)

    lanes = lax.broadcasted_iota(jnp.int32, (128, cols), 1).astype(F32)
    def localize(which):
      for t, (tr, tc) in enumerate(tiles):
        if tr not in which:
            continue
        pack = opack if (tr, tc) == (0, 0) else orecv.at[MOVES.index((-tr, -tc))]
        spots = pack[members : members + 8].T
        gap = lanes - (spots[:, 4:5] + float(tc * cols))
        near = gap * gap / float(CUT * CUT)
        gap = lanes - (spots[:, 3:4] + float(tr * rows))
        base = 1.0 - gap * gap / float(CUT * CUT)
        for r in range(rows):
            if (tr == -1 and r >= CUT - 1) or (tr == 1 and r <= rows - CUT):
                continue
            m = jnp.maximum(0.0, base[:, r : r + 1] - near)
            k0 = t * 128 - near_span(r)[0]
            local[r, k0 : k0 + 128] = (m * m).astype(BF16)

    localize((0,))
    lev_sum.wait_recv()

    weight_total = float(members * total_levels)
    sq = (sums[0] + speer[0]) / weight_total + EPS
    q0, q1, q2, q3 = [(sums[k] + speer[k]) / weight_total for k in range(1, 5)]
    q0 = pltpu.roll(q0, STEP, 1)
    top = extent - STEP
    s_here, s_below = sq[0:top], sq[STEP:extent]
    g0 = q0[0:top] / jnp.sqrt(s_here * pltpu.roll(s_below, STEP, 1))
    g1 = q1[0:top] / jnp.sqrt(s_here * s_below)
    g2 = q2[0:top] / jnp.sqrt(s_here * pltpu.roll(s_below, wide - STEP, 1))
    g3 = q3[0:top] / jnp.sqrt(s_here * pltpu.roll(s_here, wide - STEP, 1))
    up, dn = slice(0, top - STEP), slice(STEP, top)
    channels = (
        pltpu.roll(g2[up], STEP, 1),
        g1[up],
        pltpu.roll(g0[up], wide - STEP, 1),
        pltpu.roll(g3[dn], STEP, 1),
        g3[dn],
        g0[dn],
        g1[dn],
        g2[dn],
    )
    for k, channel in enumerate(channels):
        feat[:, k, :] = channel

    def conv_row(x, wh, ws, lanes):
        patch = jnp.concatenate([pltpu.roll(x, 1, 1), x, pltpu.roll(x, wide - 1, 1)], 0)
        high, low = split_two(patch[:, 0:lanes])
        z = dot(ws, high)
        return z[0:96] + z[96:192] + dot(wh, low)

    z1 = [conv_row(feat[i], w1h, w1s, wide) for i in range(3)]
    z2 = []
    tapers = []
    for i in range(rows + 2):
        h = z1[0][0:32] + z1[1][32:64] + z1[2][64:96]
        if i + 3 < rows + 4:
            z1 = [z1[1], z1[2], conv_row(feat[i + 3], w1h, w1s, wide)]
        row_at = gx * rows + (i - 1)
        keep = col_in & (row_at >= 0) & (row_at < gxn * rows)
        h = jnp.where(keep, jnp.maximum(h + b1, 0.0), 0.0)
        z2.append(conv_row(h, w2h, w2s, cols))
        if len(z2) == 3:
            out = z2[0][0:32] + z2[1][32:64] + z2[2][64:96]
            out = jnp.maximum(out + b2, 0.0)
            tapers.append(jnp.sum(out * hw, axis=0, keepdims=True) + hb)
            z2 = z2[1:]
    logits = jnp.concatenate(tapers, 0)
    taper = 1.0 / (1.0 + jnp.exp(-logits))
    taper_ref[...] = taper

    for k in range(len(others)):
        stat_copy(k).wait_recv()
    tot = stat[...]
    for k in range(len(others)):
        tot = tot + srecv[k]
    tot = jnp.sum(tot, axis=1, keepdims=True)
    inflation = tot[0:1] / (tot[1:2] + tot[2:3])
    gain = jnp.where(on, misfit / (inflation * spread + error), 0.0)
    at_obs = sum(dot(p, onehot) for p in split_three(taper))
    place = lax.broadcasted_iota(jnp.int32, (rows, 128), 0).astype(F32)
    at_obs = jnp.sum(jnp.where(place == row_o, at_obs, 0.0), axis=0, keepdims=True)
    weight = at_obs * gain / (members - 1)
    wown[...] = jnp.broadcast_to(weight, (8, 128))
    start_all(wt_copy)
    localize((-1, 1))
    recv_all(wt_copy)
    for t, (tr, tc) in enumerate(tiles):
        d = None if (tr, tc) == (0, 0) else MOVES.index((-tr, -tc))
        pack = opack if d is None else orecv.at[d]
        w = weight if d is None else wrecv[d, 0:1]
        anom = pack[0:members]
        for l in range(2):
            ratio = (first + float(l) - pack[members + 2 : members + 3]) / VCUT
            vert = jnp.maximum(0.0, 1.0 - ratio * ratio)
            near_coef = (vert * vert * w) * anom
            hid[l * members : (l + 1) * members, t * 128 : t * 128 + 128] = near_coef
    coef[...] = hid[...].astype(BF16)

    for r in range(rows):
        k0, k1 = near_span(r)
        w = dot(coef[:, k0:k1], local[r, 0 : k1 - k0])
        prod = main[RIM + r] * w
        scale = inflation * taper[r : r + 1]
        for l in range(2):
            part = jnp.sum(prod[l * members : (l + 1) * members], axis=0, keepdims=True)
            inc_ref[l * rows + r : l * rows + r + 1] = scale * part

    sent_all(halo_copy)
    sent_all(obs_copy)
    sent_all(wt_copy)
    for k in range(len(others)):
        stat_copy(k).wait_send()
    lev_obs.wait_send()
    lev_sum.wait_send()


def per_device(
    anomaly_codes,
    block_scales,
    background,
    obs_values,
    obs_error,
    obs_cell,
    obs_level,
    obs_count,
    conv1_weight,
    conv1_bias,
    conv2_weight,
    conv2_bias,
    head_weight,
    head_bias,
):
    members, levs, rows, cols = anomaly_codes.shape
    gxn, gyn = lax.axis_size("gx"), lax.axis_size("gy")
    both = members * levs
    scales = block_scales.transpose(1, 2, 3, 0)
    row = lambda v: v.reshape(1, -1)
    args = (
        anomaly_codes,
        scales,
        background,
        obs_values,
        obs_error,
        obs_cell,
        obs_level,
        obs_count,
        conv1_weight,
        conv2_weight,
        row(conv1_bias),
        row(conv2_bias),
        row(head_weight),
        row(head_bias),
    )
    vm = lambda *s, dtype=F32: pltpu.VMEM(s, dtype)
    sem = lambda n: pltpu.SemaphoreType.DMA((n,))
    extent = rows + 2 * RIM
    tiles = gxn * gyn - 1
    inc, taper = pl.pallas_call(
        functools.partial(kernel, gxn, gyn, members),
        out_shape=(
            jax.ShapeDtypeStruct((levs * rows, cols), F32),
            jax.ShapeDtypeStruct((rows, cols), F32),
        ),
        in_specs=[pl.BlockSpec(memory_space=pltpu.HBM)] * len(args),
        out_specs=[pl.BlockSpec(memory_space=pltpu.VMEM)] * 2,
        scratch_shapes=[
            vm(extent, both, cols),
            vm(extent, both, 2 * cols),
            vm(rows, 8, 128),
            vm(extent, 16, 128),
            vm(members + 8, 128),
            vm(members + 8, 128),
            vm(members + 8, 128),
            vm(8, members + 8, 128),
            vm(5, extent, 2 * cols),
            vm(5, extent, 2 * cols),
            vm(8, 128),
            vm(8, 8, 128),
            vm(8, 128),
            vm(tiles, 8, 128),
            vm(rows + 4, 8, 2 * cols),
            vm(both, 9 * 128),
            vm(both, 9 * 128, dtype=BF16),
            vm(both * rows, cols),
            vm(128, 128),
            vm(128, 128),
            vm(rows, 6 * 128, cols, dtype=BF16),
            vm(extent, both, 2 * cols),
            *[vm(*x.shape, dtype=x.dtype) for x in args],
            sem(len(args)),
            sem(8),
            sem(8),
            sem(8),
            sem(8),
            sem(8),
            sem(8),
            sem(tiles),
            sem(tiles),
            sem(2),
            sem(2),
        ],
        compiler_params=pltpu.CompilerParams(
            collective_id=0, has_side_effects=True, vmem_limit_bytes=62 * 1024 * 1024
        ),
    )(*args)
    return inc.reshape(levs, rows, cols), taper


def solution(mesh):
    in_specs = (
        P(None, "lev", ("groups", "gx"), "gy"),
        P(None, "lev", ("groups", "gx"), "gy"),
        P("lev", ("groups", "gx"), "gy"),
        P(("groups", "gx"), "gy", None),
        P(("groups", "gx"), "gy", None),
        P(("groups", "gx"), "gy", None),
        P(("groups", "gx"), "gy", None),
        P(("groups", "gx"), "gy"),
        P(),
        P(),
        P(),
        P(),
        P(),
        P(),
    )
    out_specs = (P("lev", ("groups", "gx"), "gy"), P(("groups", "gx"), "gy"))
    return jax.shard_map(
        per_device, mesh=mesh, in_specs=in_specs, out_specs=out_specs, check_vma=False
    )
```
